256 devices in a mesh: row: 16 (over z, x_lo), col: 16 (over y, x_hi, core).
Axes of the slice: x: 4 (x_hi: 2, x_lo: 2; x = x_hi * 2 + x_lo), y: 4, z: 8, core: 2. Of those that a mesh axis runs over, the one named last changes fastest.
Arguments:
- fraction: float32 [128, 128, 2048], P('row', 'col'), may hold values from 0 to 1
- flow_x: float32 [128, 128, 2048], P('row', 'col'), may hold values from -0.4 to 0.4
- flow_y: float32 [128, 128, 2048], P('row', 'col'), may hold values from -0.4 to 0.4
- flow_z: float32 [128, 128, 2048], P('row', 'col'), may hold values from -0.4 to 0.4
Outputs:
- advected: float32 [128, 128, 2048], P('row', 'col')
The draws below stay inside these ranges and needn't reach their ends.
All inputs are finite; a program needn't handle non-finite values.
Results may differ from the reference program's by a relative error of at most 0.0003.
Values sent between devices are 32-bit elements; how exact they have to be, the bound alone decides.
No kernel may reach another device: no remote copies, remote signals or barrier semaphores. Data moves between devices by JAX's collectives and lax.ppermute only.
A program may use at most 64 MiB of HBM per device.

```python
import jax
import jax.numpy as jnp

NX = 2048
NY = 128
NZ = 128


def level_of(key, shape, cuts, least, top_value):
    gain = 1.0
    for position, blocks in cuts:
        steps = jax.random.uniform(jax.random.fold_in(jax.random.fold_in(key, 6), position), (blocks,), jnp.float32, least / len(cuts), top_value / len(cuts))
        gain = gain * jnp.repeat(jnp.exp(steps), shape[position] // blocks).reshape((-1,) + (1,) * (len(shape) - 1 - position))
    return gain


def setup_inputs(seed: int = 0) -> dict:
    arg_keys = jax.random.split(jax.random.key(seed), 5)
    return {
        "fraction": jnp.clip(1.0 * jax.random.uniform(arg_keys[0], (NY, NZ, NX), jnp.float32) ** level_of(arg_keys[0], (NY, NZ, NX), ((0, 16), (1, 16)), -0.2, 0.2), 0.0, 1.0),
        "flow_x": jnp.clip(jax.random.uniform(arg_keys[1], (NY, NZ, NX), jnp.float32, -0.4, 0.4) * level_of(arg_keys[1], (NY, NZ, NX), ((0, 16), (1, 16)), -0.4, 0.0), -0.4, 0.4),
        "flow_y": jnp.clip(jax.random.uniform(arg_keys[2], (NY, NZ, NX), jnp.float32, -0.4, 0.4) * level_of(arg_keys[2], (NY, NZ, NX), ((0, 16), (1, 16)), -0.4, 0.0), -0.4, 0.4),
        "flow_z": jnp.clip(jax.random.uniform(arg_keys[3], (NY, NZ, NX), jnp.float32, -0.4, 0.4) * level_of(arg_keys[3], (NY, NZ, NX), ((0, 16), (1, 16)), -0.4, 0.0), -0.4, 0.4),
    }


def face_flux(field, courant, direction):
    normal = jnp.roll(field, -1, direction) - jnp.roll(field, 1, direction)
    field_below = jnp.roll(field, 1, direction)
    normal_below = jnp.roll(normal, 1, direction)
    forward = courant >= 0.0
    donor_value = jnp.where(forward, field_below, field)
    slope_side = jnp.where(forward, normal_below, -normal)
    reach = jnp.abs(courant)
    weight = jax.nn.sigmoid(20.0 * slope_side)
    volume = weight * jnp.minimum(donor_value, reach) + (1.0 - weight) * jnp.maximum(0.0, reach - 1.0 + donor_value)
    return jnp.where(forward, volume, -volume)


def advance(field, courant, indicator, direction):
    flux = face_flux(field, courant, direction)
    outflow = jnp.roll(flux, -1, direction) - flux
    spread = jnp.roll(courant, -1, direction) - courant
    return field - outflow + indicator * spread


def reference(fraction, flow_x, flow_y, flow_z):
    indicator = jnp.where(fraction > 0.5, 1.0, 0.0).astype(fraction.dtype)
    first = advance(fraction, flow_x, indicator, 2)
    second = advance(first, flow_y, indicator, 0)
    return advance(second, flow_z, indicator, 1)
```

```python
import jax
import jax.numpy as jnp
from jax import lax
from jax.experimental import pallas as pl
from jax.experimental.pallas import tpu as pltpu
from jax.sharding import PartitionSpec as P


def face_flux(two_below, below, here, above, courant):
    forward = courant >= 0.0
    donor = jnp.where(forward, below, here)
    slope = jnp.where(forward, here - two_below, below - above)
    reach = jnp.abs(courant)
    least = jnp.minimum(donor, reach)
    most = jnp.maximum(0.0, reach - 1.0 + donor)
    tilt = jnp.tanh(10.0 * slope)
    volume = 0.5 * ((least + most) + tilt * (least - most))
    return jnp.where(forward, volume, -volume)


def updated(here, flux, next_flux, courant, next_courant, start):
    spread = jnp.where(start > 0.5, next_courant - courant, 0.0)
    return here - (next_flux - flux) + spread


def x_sweep(fraction, flow_x, flow_y, first, upward, downward):
    rows, _, length = fraction.shape

    def row(i, _):
        here = fraction[i]
        courant = flow_x[i]
        below = pltpu.roll(here, 1, 1)
        two_below = pltpu.roll(here, 2, 1)
        above = pltpu.roll(here, length - 1, 1)
        flux = face_flux(two_below, below, here, above, courant)
        first[i] = updated(
            here,
            flux,
            pltpu.roll(flux, length - 1, 1),
            courant,
            pltpu.roll(courant, length - 1, 1),
            here,
        )
        return _

    lax.fori_loop(0, rows, row, None)
    upward[...] = first[rows - 2 :]
    downward[:2] = first[:2]
    downward[2] = flow_y[0]


def y_sweep(first, flow_y, fraction, flow_z, lower, upper, second, upward, downward):
    rows, columns, length = first.shape

    def tile(t, _):
        at = pl.ds(pl.multiple_of(t * 128, 128), 128)
        cells = (
            [lower[0, :, at], lower[1, :, at]]
            + [first[i, :, at] for i in range(rows)]
            + [upper[0, :, at], upper[1, :, at]]
        )
        flows = [flow_y[i, :, at] for i in range(rows)] + [upper[2, :, at]]
        flux = face_flux(*cells[:4], flows[0])
        for i in range(rows):
            next_flux = face_flux(*cells[i + 1 : i + 5], flows[i + 1])
            result = updated(
                cells[i + 2], flux, next_flux, flows[i], flows[i + 1], fraction[i, :, at]
            )
            flux = next_flux
            second[i, :, at] = result
            upward[0, i : i + 1, at] = result[columns - 2 : columns - 1]
            upward[1, i : i + 1, at] = result[columns - 1 :]
            downward[0, i : i + 1, at] = result[:1]
            downward[1, i : i + 1, at] = result[1:2]
            downward[2, i : i + 1, at] = flow_z[i, :1, at]
        return _

    lax.fori_loop(0, length // 128, tile, None)


def z_sweep(second, flow_z, fraction, own, lower, upper, out, last_flux):
    rows, columns, length = second.shape
    chunk = 512
    place = lax.broadcasted_iota(jnp.int32, (columns, chunk), 0)
    bottom = place == 0
    top = place == columns - 1

    for k in range(length // chunk):
        at = slice(k * chunk, (k + 1) * chunk)
        last_flux[:, at] = face_flux(
            own[0, :, at], own[1, :, at], upper[0, :, at], upper[1, :, at], upper[2, :, at]
        )

    for k in range(length // chunk):
        at = slice(k * chunk, (k + 1) * chunk)
        for i in range(rows):
            here = second[i, :, at]
            courant = flow_z[i, :, at]
            below = jnp.where(bottom, lower[1, i : i + 1, at], pltpu.roll(here, 1, 0))
            two_below = jnp.where(bottom, lower[0, i : i + 1, at], pltpu.roll(below, 1, 0))
            above = jnp.where(top, upper[0, i : i + 1, at], pltpu.roll(here, columns - 1, 0))
            flux = face_flux(two_below, below, here, above, courant)
            next_flux = jnp.where(top, last_flux[i : i + 1, at], pltpu.roll(flux, columns - 1, 0))
            next_courant = jnp.where(
                top, upper[2, i : i + 1, at], pltpu.roll(courant, columns - 1, 0)
            )
            out[i, :, at] = updated(
                here, flux, next_flux, courant, next_courant, fraction[i, :, at]
            )


def in_vmem(n):
    return [pl.BlockSpec(memory_space=pltpu.VMEM)] * n


def per_device(n_row, n_col, fraction, flow_x, flow_y, flow_z):
    block, dtype = fraction.shape, fraction.dtype
    rows, columns, length = block
    whole = jax.ShapeDtypeStruct(block, dtype)
    params = pltpu.CompilerParams(vmem_limit_bytes=32 * 1024 * 1024)

    def slabs(n, width):
        return jax.ShapeDtypeStruct((n, width, length), dtype)

    up = lambda n: [(i, (i + 1) % n) for i in range(n)]
    down = lambda n: [(i, (i - 1) % n) for i in range(n)]

    first, upward, downward = pl.pallas_call(
        x_sweep,
        out_shape=(whole, slabs(2, columns), slabs(3, columns)),
        in_specs=in_vmem(3),
        out_specs=in_vmem(3),
        compiler_params=params,
    )(fraction, flow_x, flow_y)
    lower = lax.ppermute(upward, "row", up(n_row))
    upper = lax.ppermute(downward, "row", down(n_row))
    second, upward, downward = pl.pallas_call(
        y_sweep,
        out_shape=(whole, slabs(2, rows), slabs(3, rows)),
        in_specs=in_vmem(6),
        out_specs=in_vmem(3),
        compiler_params=params,
    )(first, flow_y, fraction, flow_z, lower, upper)
    lower = lax.ppermute(upward, "col", up(n_col))
    upper = lax.ppermute(downward, "col", down(n_col))
    return pl.pallas_call(
        z_sweep,
        out_shape=whole,
        in_specs=in_vmem(6),
        out_specs=pl.BlockSpec(memory_space=pltpu.VMEM),
        scratch_shapes=[pltpu.VMEM((rows, length), dtype)],
        compiler_params=params,
    )(second, flow_z, fraction, upward, lower, upper)


def solution(mesh):
    spec = P("row", "col", None)

    def step(fraction, flow_x, flow_y, flow_z):
        return per_device(
            mesh.shape["row"], mesh.shape["col"], fraction, flow_x, flow_y, flow_z
        )

    return jax.shard_map(
        step, mesh=mesh, in_specs=(spec,) * 4, out_specs=spec, check_vma=False
    )
```

```python
import jax
import jax.numpy as jnp
from jax import lax
from jax.experimental import pallas as pl
from jax.experimental.pallas import tpu as pltpu
from jax.sharding import PartitionSpec as P

LANES = 128


def face_flux(two_below, below, here, above, courant):
    forward = courant >= 0.0
    donor = jnp.where(forward, below, here)
    slope = jnp.where(forward, here - two_below, below - above)
    return donor_flux(forward, donor, slope, courant)


def donor_flux(forward, donor, slope, courant):
    reach = jnp.abs(courant)
    least = jnp.minimum(donor, reach)
    most = jnp.maximum(0.0, reach - 1.0 + donor)
    tilt = jnp.tanh(10.0 * slope)
    return jnp.where(forward, 0.5, -0.5) * ((least + most) + tilt * (least - most))


def updated(here, flux, next_flux, courant, next_courant, start):
    spread = jnp.where(start > 0.5, next_courant - courant, 0.0)
    return here - (next_flux - flux) + spread


def x_sweep_row(here, courant):
    length = here.shape[1]
    below = pltpu.roll(here, 1, 1)
    two_below = pltpu.roll(here, 2, 1)
    above = pltpu.roll(here, length - 1, 1)
    flux = face_flux(two_below, below, here, above, courant)
    from_below = flux - jnp.where(below > 0.5, courant, 0.0)
    to_above = flux - jnp.where(here > 0.5, courant, 0.0)
    return here + (to_above - pltpu.roll(from_below, length - 1, 1))


def x_far(fraction, flow_x, flow_y, flow_z, far, courant_y, courant_z, cells, flows, sems):
    far_row = lax.rem(lax.axis_index("row"), 2) * (fraction.shape[0] - 2)
    at = pl.ds(far_row, 2)
    loads = [
        pltpu.make_async_copy(source, into, sems.at[n])
        for n, (source, into) in enumerate(
            (
                (fraction.at[at], cells),
                (flow_x.at[at], flows),
                (flow_y.at[0], courant_y),
                (flow_z.at[:, 0], courant_z),
            )
        )
    ]
    for load in loads:
        load.start()
    loads[0].wait()
    loads[1].wait()
    for i in range(2):
        far[i] = x_sweep_row(cells[i], flows[i])
    loads[2].wait()
    loads[3].wait()


def x_near(fraction, flow_x, far, near):
    del far
    near_row = lax.rem(lax.axis_index("row") + 1, 2) * (fraction.shape[0] - 2)
    for i in range(2):
        near[i] = x_sweep_row(fraction[near_row + i], flow_x[near_row + i])


def x_middle(fraction, flow_x, near, flow_z, middle, inner_z, sems):
    del near
    loads = [
        pltpu.make_async_copy(flow_z.at[:, column], inner_z.at[n], sems.at[n])
        for n, column in enumerate((1, flow_z.shape[1] - 1))
    ]
    for load in loads:
        load.start()
    for i in range(middle.shape[0]):
        middle[i] = x_sweep_row(fraction[i + 2], flow_x[i + 2])
    for load in loads:
        load.wait()


def y_sweep(
    near, near_side, far, far_side, courant_y, middle, flow_y, fraction,
    second, core, chip,
):
    rows, columns, length = second.shape
    odd = lax.rem(lax.axis_index("row"), 2) == 1
    odd_core = lax.rem(lax.axis_index("col"), 2) == 1

    def tile(t, _):
        at = pl.ds(pl.multiple_of(t * LANES, LANES), LANES)

        def ordered(a, b):
            return lax.select(odd, a, b), lax.select(odd, b, a)

        below, above = zip(*(ordered(near_side[i, :, at], far_side[i, :, at]) for i in range(2)))
        low, high = zip(*(ordered(near[i, :, at], far[i, :, at]) for i in range(2)))
        cells = [*below, *low, *(middle[i, :, at] for i in range(rows - 4)), *high, *above]
        flows = [flow_y[i, :, at] for i in range(rows)] + [courant_y[:, at]]
        flux = face_flux(*cells[:4], flows[0])
        for i in range(rows):
            next_flux = face_flux(*cells[i + 1 : i + 5], flows[i + 1])
            result = updated(
                cells[i + 2], flux, next_flux, flows[i], flows[i + 1], fraction[i, :, at]
            )
            flux = next_flux
            second[i, :, at] = result
            for m in range(2):
                up, down = result[columns - 2 + m : columns - 1 + m], result[m : m + 1]
                core[m, i : i + 1, at] = lax.select(odd_core, down, up)
                chip[m, i : i + 1, at] = lax.select(odd_core, up, down)
        return _

    lax.fori_loop(0, length // LANES, tile, None, unroll=2)


CHUNK = 512


def z_inner(second, flow_z, fraction, courant_z, base, inner_cells):
    rows, columns, length = second.shape
    place = lax.broadcasted_iota(jnp.int32, (columns, CHUNK), 0)
    top = place == columns - 1
    inner = (place >= 2) & (place <= columns - 2)
    for i in range(rows):
        for j in range(length // CHUNK):
            at = slice(j * CHUNK, (j + 1) * CHUNK)
            here = second[i, :, at]
            courant = flow_z[i, :, at]
            flux = face_flux(
                pltpu.roll(here, 2, 0),
                pltpu.roll(here, 1, 0),
                here,
                pltpu.roll(here, columns - 1, 0),
                courant,
            )
            flux = jnp.where(inner, flux, 0.0)
            next_courant = jnp.where(
                top, courant_z[i : i + 1, at], pltpu.roll(courant, columns - 1, 0)
            )
            base[i, :, at] = updated(
                here, flux, pltpu.roll(flux, columns - 1, 0), courant, next_courant,
                fraction[i, :, at],
            )
            inner_cells[0, i : i + 1, at] = here[2:3]
            inner_cells[1, i : i + 1, at] = here[columns - 3 : columns - 2]


def z_outer(
    chip, chip_side, core, core_side, base, inner_cells, inner_z, own_z, courant_z, out,
    part, change, sems,
):
    rows, columns, length = base.shape
    odd_core = lax.rem(lax.axis_index("col"), 2) == 1
    place = lax.broadcasted_iota(jnp.int32, (columns, CHUNK), 0)
    pieces = [slice(j * CHUNK, (j + 1) * CHUNK) for j in range(length // CHUNK)]

    for at in pieces:

        def ordered(a, b, at=at):
            pairs = [(a[m, :, at], b[m, :, at]) for m in range(2)]
            return [lax.select(odd_core, x, y) for x, y in pairs], [
                lax.select(odd_core, y, x) for x, y in pairs
            ]

        below, above = ordered(core_side, chip_side)
        low, high = ordered(core, chip)
        after_low, before_high = inner_cells[0, :, at], inner_cells[1, :, at]
        flux = [
            face_flux(*below, *low, own_z[:, at]),
            face_flux(below[1], *low, after_low, inner_z[0, :, at]),
            face_flux(before_high, *high, above[0], inner_z[1, :, at]),
            face_flux(*high, *above, courant_z[:, at]),
        ]
        change[0, :, at] = flux[0] - flux[1]
        change[1, :, at] = flux[1]
        change[2, :, at] = -flux[2]
        change[3, :, at] = flux[2] - flux[3]

    stores = []
    for i in range(rows):
        for at in pieces:
            value = jnp.zeros((columns, CHUNK), base.dtype)
            for n, column in enumerate((0, 1, columns - 2, columns - 1)):
                value = jnp.where(place == column, change[n, i : i + 1, at], value)
            part[i, :, at] = base[i, :, at] + value
        stores.append(pltpu.make_async_copy(part.at[i], out.at[i], sems.at[i]))
        stores[-1].start()
    for store in stores:
        store.wait()


def per_device(n_row, n_col, fraction, flow_x, flow_y, flow_z):
    block, dtype = fraction.shape, fraction.dtype
    rows, columns, length = block
    vmem = pl.BlockSpec(memory_space=pltpu.VMEM)
    hbm = pl.BlockSpec(memory_space=pltpu.HBM)
    params = pltpu.CompilerParams(vmem_limit_bytes=16 * 1024 * 1024)
    dma = pltpu.SemaphoreType.DMA

    def array(*shape):
        return jax.ShapeDtypeStruct(shape, dtype)

    def with_above(n):
        return [(i, i ^ 1) for i in range(n)]

    def down(n):
        return [(i, (i - 1) % n) for i in range(n)]

    def with_below(n):
        return [(i, ((i + 1 ^ 1) - 1) % n) for i in range(n)]

    inputs = [
        pltpu.with_memory_space_constraint(x, pltpu.HBM) for x in (fraction, flow_x, flow_y, flow_z)
    ]
    far, own_y, own_z = pl.pallas_call(
        x_far,
        out_shape=(array(2, columns, length), array(columns, length), array(rows, length)),
        in_specs=[hbm] * 4,
        out_specs=[vmem] * 3,
        scratch_shapes=[
            pltpu.VMEM((2, columns, length), dtype),
            pltpu.VMEM((2, columns, length), dtype),
            dma((4,)),
        ],
        compiler_params=params,
        name="x_far",
    )(*inputs)
    far_side = lax.ppermute(far, "row", with_below(n_row))
    near = pl.pallas_call(
        x_near,
        out_shape=array(2, columns, length),
        in_specs=[vmem] * 3,
        out_specs=vmem,
        compiler_params=params,
        name="x_near",
    )(fraction, flow_x, far)
    near_side = lax.ppermute(near, "row", with_above(n_row))
    courant_y = lax.ppermute(own_y, "row", down(n_row))
    courant_z = lax.ppermute(own_z, "col", down(n_col))
    middle, inner_z = pl.pallas_call(
        x_middle,
        out_shape=(array(rows - 4, columns, length), array(2, rows, length)),
        in_specs=[vmem] * 3 + [hbm],
        out_specs=[vmem] * 2,
        scratch_shapes=[dma((2,))],
        compiler_params=params,
        name="x_middle",
    )(fraction, flow_x, near, inputs[3])
    second, core, chip = pl.pallas_call(
        y_sweep,
        out_shape=(array(*block), array(2, rows, length), array(2, rows, length)),
        in_specs=[vmem] * 8,
        out_specs=[vmem] * 3,
        compiler_params=params,
        cost_estimate=pl.CostEstimate(flops=10**10, bytes_accessed=10**7, transcendentals=0),
        name="y_sweep",
    )(near, near_side, far, far_side, courant_y, middle, flow_y, fraction)
    chip_side = lax.ppermute(chip, "col", with_below(n_col))
    core_side = lax.ppermute(core, "col", with_above(n_col))
    base, inner_cells = pl.pallas_call(
        z_inner,
        out_shape=(array(*block), array(2, rows, length)),
        in_specs=[vmem] * 4,
        out_specs=[vmem] * 2,
        compiler_params=params,
        cost_estimate=pl.CostEstimate(flops=10**10, bytes_accessed=10**7, transcendentals=0),
        name="z_inner",
    )(second, flow_z, fraction, courant_z)
    return pl.pallas_call(
        z_outer,
        out_shape=array(*block),
        in_specs=[vmem] * 9,
        out_specs=hbm,
        scratch_shapes=[
            pltpu.VMEM(block, dtype),
            pltpu.VMEM((4, rows, length), dtype),
            dma((rows,)),
        ],
        compiler_params=params,
        name="z_outer",
    )(chip, chip_side, core, core_side, base, inner_cells, inner_z, own_z, courant_z)


def solution(mesh):
    spec = P("row", "col", None)

    def step(fraction, flow_x, flow_y, flow_z):
        return per_device(
            mesh.shape["row"], mesh.shape["col"], fraction, flow_x, flow_y, flow_z
        )

    return jax.shard_map(
        step, mesh=mesh, in_specs=(spec,) * 4, out_specs=spec, check_vma=False
    )
```

```python
import jax
import jax.numpy as jnp
from jax import lax
from jax.experimental import pallas as pl
from jax.experimental.pallas import tpu as pltpu
from jax.sharding import PartitionSpec as P

LANES = 128
CHUNK = 512


def face_flux(two_below, below, here, above, courant):
    forward = courant >= 0.0
    donor = jnp.where(forward, below, here)
    slope = jnp.where(forward, here - two_below, below - above)
    return donor_flux(forward, donor, slope, courant)


def donor_flux(forward, donor, slope, courant):
    reach = jnp.abs(courant)
    least = jnp.minimum(donor, reach)
    most = jnp.maximum(0.0, reach - 1.0 + donor)
    tilt = jnp.tanh(10.0 * slope)
    return jnp.where(forward, 0.5, -0.5) * ((least + most) + tilt * (least - most))


def updated(here, flux, next_flux, courant, next_courant, start):
    spread = jnp.where(start > 0.5, next_courant - courant, 0.0)
    return here - (next_flux - flux) + spread


def x_sweep_row(here, courant):
    length = here.shape[1]
    below = pltpu.roll(here, 1, 1)
    two_below = pltpu.roll(here, 2, 1)
    above = pltpu.roll(here, length - 1, 1)
    flux = face_flux(two_below, below, here, above, courant)
    from_below = flux - jnp.where(below > 0.5, courant, 0.0)
    to_above = flux - jnp.where(here > 0.5, courant, 0.0)
    return here + (to_above - pltpu.roll(from_below, length - 1, 1))


def x_columns(
    fraction, flow_x, flow_y, flow_z, first, start, courant, upward, downward, own_y, own_z,
    flows, sems,
):
    rows, columns, _ = fraction.shape
    column = lax.rem(lax.axis_index("col"), 2) * (columns - 2)
    loads = [
        pltpu.make_async_copy(source.at[:, column + m], into.at[m], sems.at[2 * n + m])
        for n, (source, into) in enumerate(((fraction, start), (flow_x, flows), (flow_y, courant)))
        for m in range(2)
    ]
    loads.append(pltpu.make_async_copy(flow_y.at[0], own_y, sems.at[6]))
    loads.append(pltpu.make_async_copy(flow_z.at[:, 0], own_z, sems.at[7]))
    for load in loads:
        load.start()
    for load in loads[:4]:
        load.wait()
    for m in range(2):
        result = x_sweep_row(start[m], flows[m])
        first[m] = result
        for i in range(2):
            upward[i, m : m + 1] = result[rows - 2 + i : rows - 1 + i]
            downward[i, m : m + 1] = result[i : i + 1]
    for load in loads[4:]:
        load.wait()
    for m in range(2):
        downward[2, m : m + 1] = courant[m, :1]


def x_rows(fraction, flow_x, own_y, high, low, upward, downward):
    rows, columns, _ = fraction.shape
    odd_core = lax.rem(lax.axis_index("col"), 2) == 1
    pairs = columns // 2 - 1

    def put(message, i, row):
        for p in range(pairs):
            message[i * pairs + p] = lax.select(
                odd_core, row[2 * p : 2 * p + 2], row[2 * p + 2 : 2 * p + 4]
            )

    put(downward, 2, own_y[...])
    for mine, message, start in ((low, downward, 0), (high, upward, rows - 2)):
        for i in range(2):
            mine[i] = x_sweep_row(fraction[start + i], flow_x[start + i])
            put(message, i, mine[i])


def x_middle(fraction, flow_x, chip, middle):
    del chip
    for i in range(middle.shape[0]):
        middle[i] = x_sweep_row(fraction[i + 2], flow_x[i + 2])


def y_columns(first, start, courant, high, lower, upper, own_z, chip, own_z_out):
    _, rows, length = first.shape
    own_z_out[...] = own_z[...]
    place = lax.broadcasted_iota(jnp.int32, (rows, CHUNK), 0)
    bottom = place == 0
    top = place == rows - 1
    for j in range(length // CHUNK):
        at = slice(j * CHUNK, (j + 1) * CHUNK)
        last_flux = face_flux(
            high[0, :, at], high[1, :, at], upper[0, :, at], upper[1, :, at], upper[2, :, at]
        )
        for m in range(2):
            one = slice(m, m + 1)
            here, flow = first[m, :, at], courant[m, :, at]
            below = jnp.where(bottom, lower[1, one, at], pltpu.roll(here, 1, 0))
            two_below = jnp.where(bottom, lower[0, one, at], pltpu.roll(below, 1, 0))
            above = jnp.where(top, upper[0, one, at], pltpu.roll(here, rows - 1, 0))
            flux = face_flux(two_below, below, here, above, flow)
            next_flux = jnp.where(top, last_flux[one], pltpu.roll(flux, rows - 1, 0))
            next_flow = jnp.where(top, upper[2, one, at], pltpu.roll(flow, rows - 1, 0))
            chip[m, :, at] = updated(here, flux, next_flux, flow, next_flow, start[m, :, at])


def y_sweep(
    high, lower_pairs, low, upper_pairs, lower_edge, upper_edge, middle, flow_y, fraction,
    second, core, halo,
):
    rows, columns, length = second.shape
    odd_core = lax.rem(lax.axis_index("col"), 2) == 1
    pairs = columns // 2 - 1
    for edge, rest, slabs in ((lower_edge, lower_pairs, (0, 1)), (upper_edge, upper_pairs, (2, 3, 4))):
        for m, slab in enumerate(slabs):
            others = [rest[m * pairs + p] for p in range(pairs)]
            ends = [edge[m], *others], [*others, edge[m]]
            for p in range(pairs + 1):
                halo[slab, 2 * p : 2 * p + 2] = lax.select(odd_core, ends[1][p], ends[0][p])

    def tile(t, _):
        at = pl.ds(pl.multiple_of(t * LANES, LANES), LANES)

        def pair(ref, start=0):
            return [ref[start + i, :, at] for i in range(2)]

        inner = [middle[i, :, at] for i in range(rows - 4)]
        cells = pair(halo) + pair(low) + inner + pair(high) + pair(halo, 2)
        flows = [flow_y[i, :, at] for i in range(rows)] + [halo[4, :, at]]
        flux = face_flux(*cells[:4], flows[0])
        for i in range(rows):
            next_flux = face_flux(*cells[i + 1 : i + 5], flows[i + 1])
            result = updated(
                cells[i + 2], flux, next_flux, flows[i], flows[i + 1], fraction[i, :, at]
            )
            flux = next_flux
            second[i, :, at] = result
            for m in range(2):
                up, down = result[columns - 2 + m : columns - 1 + m], result[m : m + 1]
                core[m, i : i + 1, at] = lax.select(odd_core, down, up)
        return _

    lax.fori_loop(0, length // LANES, tile, None, unroll=2)


def z_inner(second, flow_z, fraction, base, inside):
    rows, columns, length = second.shape
    place = lax.broadcasted_iota(jnp.int32, (columns, CHUNK), 0)
    top = place == columns - 1
    inner = (place >= 2) & (place <= columns - 2)
    for i in range(rows):
        for j in range(length // CHUNK):
            at = slice(j * CHUNK, (j + 1) * CHUNK)
            here = second[i, :, at]
            courant = flow_z[i, :, at]
            flux = face_flux(
                pltpu.roll(here, 2, 0),
                pltpu.roll(here, 1, 0),
                here,
                pltpu.roll(here, columns - 1, 0),
                courant,
            )
            flux = jnp.where(inner, flux, 0.0)
            next_courant = jnp.where(top, 0.0, pltpu.roll(courant, columns - 1, 0))
            start = fraction[i, :, at]
            base[i, :, at] = updated(
                here, flux, pltpu.roll(flux, columns - 1, 0), courant, next_courant, start
            )
            inside[4, i : i + 1, at] = start[columns - 1 :]
            inside[0, i : i + 1, at] = here[2:3]
            inside[1, i : i + 1, at] = here[columns - 3 : columns - 2]
            inside[2, i : i + 1, at] = courant[1:2]
            inside[3, i : i + 1, at] = courant[columns - 1 :]


def z_outer(
    chip, chip_side, core, core_side, base, inside, own_z, courant_z, out,
    part, change, sems,
):
    rows, columns, length = base.shape
    odd_core = lax.rem(lax.axis_index("col"), 2) == 1
    place = lax.broadcasted_iota(jnp.int32, (columns, CHUNK), 0)
    pieces = [slice(j * CHUNK, (j + 1) * CHUNK) for j in range(length // CHUNK)]

    for at in pieces:

        def ordered(a, b, at=at):
            pairs = [(a[m, :, at], b[m, :, at]) for m in range(a.shape[0])]
            return [lax.select(odd_core, x, y) for x, y in pairs], [
                lax.select(odd_core, y, x) for x, y in pairs
            ]

        below, above = ordered(core_side, chip_side)
        low, high = ordered(core, chip)
        after_low, before_high = inside[0, :, at], inside[1, :, at]
        flux = [
            face_flux(*below, *low, own_z[:, at]),
            face_flux(below[1], *low, after_low, inside[2, :, at]),
            face_flux(before_high, *high, above[0], inside[3, :, at]),
            face_flux(*high, *above, courant_z[:, at]),
        ]
        change[0, :, at] = flux[0] - flux[1]
        change[1, :, at] = flux[1]
        change[2, :, at] = -flux[2]
        spread = jnp.where(inside[4, :, at] > 0.5, courant_z[:, at], 0.0)
        change[3, :, at] = flux[2] - flux[3] + spread

    stores = []
    for i in range(rows):
        for at in pieces:
            value = jnp.zeros((columns, CHUNK), base.dtype)
            for n, column in enumerate((0, 1, columns - 2, columns - 1)):
                value = jnp.where(place == column, change[n, i : i + 1, at], value)
            part[i, :, at] = base[i, :, at] + value
        stores.append(pltpu.make_async_copy(part.at[i], out.at[i], sems.at[i]))
        stores[-1].start()
    for store in stores:
        store.wait()


def per_device(n_row, n_col, fraction, flow_x, flow_y, flow_z):
    block, dtype = fraction.shape, fraction.dtype
    rows, columns, length = block
    vmem = pl.BlockSpec(memory_space=pltpu.VMEM)
    hbm = pl.BlockSpec(memory_space=pltpu.HBM)
    params = pltpu.CompilerParams(vmem_limit_bytes=16 * 1024 * 1024)
    dma = pltpu.SemaphoreType.DMA
    busy = pl.CostEstimate(flops=10**10, bytes_accessed=10**7, transcendentals=0)

    def array(*shape):
        return jax.ShapeDtypeStruct(shape, dtype)

    def with_above(n):
        return [(i, i ^ 1) for i in range(n)]

    def up(n):
        return [(i, (i + 1) % n) for i in range(n)]

    def down(n):
        return [(i, (i - 1) % n) for i in range(n)]

    def with_below(n):
        return [(i, ((i + 1 ^ 1) - 1) % n) for i in range(n)]

    inputs = [
        pltpu.with_memory_space_constraint(x, pltpu.HBM) for x in (fraction, flow_x, flow_y, flow_z)
    ]
    edge, side = array(2, rows, length), array(2, 2, length)
    first, start, courant, upward, downward, own_y, own_z = pl.pallas_call(
        x_columns,
        out_shape=(
            edge, edge, edge, side, array(3, 2, length), array(columns, length), array(rows, length)
        ),
        in_specs=[hbm] * 4,
        out_specs=[vmem] * 7,
        scratch_shapes=[pltpu.VMEM((2, rows, length), dtype), dma((8,))],
        compiler_params=params,
        name="x_columns",
    )(*inputs)
    column_lower = lax.ppermute(upward, "row", up(n_row))
    column_upper = lax.ppermute(downward, "row", down(n_row))
    pairs = columns // 2 - 1
    high, low, upward_pairs, downward_pairs = pl.pallas_call(
        x_rows,
        out_shape=(
            array(2, columns, length),
            array(2, columns, length),
            array(2 * pairs, 2, length),
            array(3 * pairs, 2, length),
        ),
        in_specs=[vmem] * 3,
        out_specs=[vmem] * 4,
        compiler_params=params,
        cost_estimate=busy,
        name="x_rows",
    )(fraction, flow_x, own_y)
    lower_pairs = lax.ppermute(upward_pairs, "row", up(n_row))
    upper_pairs = lax.ppermute(downward_pairs, "row", down(n_row))
    chip, own_z = pl.pallas_call(
        y_columns,
        out_shape=(edge, array(rows, length)),
        in_specs=[vmem] * 7,
        out_specs=[vmem] * 2,
        compiler_params=params,
        cost_estimate=busy,
        name="y_columns",
    )(first, start, courant, upward, column_lower, column_upper, own_z)
    chip_side = lax.ppermute(chip, "col", with_below(n_col))
    courant_z = lax.ppermute(own_z, "col", down(n_col))
    middle = pl.pallas_call(
        x_middle,
        out_shape=array(rows - 4, columns, length),
        in_specs=[vmem] * 3,
        out_specs=vmem,
        compiler_params=params,
        name="x_middle",
    )(fraction, flow_x, chip)
    second, core = pl.pallas_call(
        y_sweep,
        out_shape=(array(*block), edge),
        in_specs=[vmem] * 9,
        out_specs=[vmem] * 2,
        scratch_shapes=[pltpu.VMEM((5, columns, length), dtype)],
        compiler_params=params,
        cost_estimate=busy,
        name="y_sweep",
    )(
        high, lower_pairs, low, upper_pairs, column_lower, column_upper, middle, flow_y, fraction
    )
    core_side = lax.ppermute(core, "col", with_above(n_col))
    base, inside = pl.pallas_call(
        z_inner,
        out_shape=(array(*block), array(5, rows, length)),
        in_specs=[vmem] * 3,
        out_specs=[vmem] * 2,
        compiler_params=params,
        cost_estimate=busy,
        name="z_inner",
    )(second, flow_z, fraction)
    return pl.pallas_call(
        z_outer,
        out_shape=array(*block),
        in_specs=[vmem] * 8,
        out_specs=hbm,
        scratch_shapes=[
            pltpu.VMEM(block, dtype),
            pltpu.VMEM((4, rows, length), dtype),
            dma((rows,)),
        ],
        compiler_params=params,
        name="z_outer",
    )(chip, chip_side, core, core_side, base, inside, own_z, courant_z)


def solution(mesh):
    spec = P("row", "col", None)

    def step(fraction, flow_x, flow_y, flow_z):
        return per_device(
            mesh.shape["row"], mesh.shape["col"], fraction, flow_x, flow_y, flow_z
        )

    return jax.shard_map(
        step, mesh=mesh, in_specs=(spec,) * 4, out_specs=spec, check_vma=False
    )
```

```python
import jax
import jax.numpy as jnp
from jax import lax
from jax.experimental import pallas as pl
from jax.experimental.pallas import tpu as pltpu
from jax.sharding import PartitionSpec as P

LANES = 128
CHUNK = 512


def face_flux(two_below, below, here, above, courant):
    forward = courant >= 0.0
    donor = jnp.where(forward, below, here)
    slope = jnp.where(forward, here - two_below, below - above)
    return donor_flux(forward, donor, slope, courant)


def donor_flux(forward, donor, slope, courant):
    reach = jnp.abs(courant)
    least = jnp.minimum(donor, reach)
    most = jnp.maximum(0.0, reach - 1.0 + donor)
    tilt = jnp.tanh(10.0 * slope)
    return jnp.where(forward, 0.5, -0.5) * ((least + most) + tilt * (least - most))


def updated(here, flux, next_flux, courant, next_courant, start):
    spread = jnp.where(start > 0.5, next_courant - courant, 0.0)
    return here - (next_flux - flux) + spread


def x_sweep_row(here, courant):
    length = here.shape[1]
    below = pltpu.roll(here, 1, 1)
    two_below = pltpu.roll(here, 2, 1)
    above = pltpu.roll(here, length - 1, 1)
    flux = face_flux(two_below, below, here, above, courant)
    from_below = flux - jnp.where(below > 0.5, courant, 0.0)
    to_above = flux - jnp.where(here > 0.5, courant, 0.0)
    return here + (to_above - pltpu.roll(from_below, length - 1, 1))


def x_columns(
    fraction, flow_x, flow_y, flow_z, first, start, courant, near, far, own_y, own_z, flows, sems,
):
    rows, columns, _ = fraction.shape
    column = lax.rem(lax.axis_index("col"), 2) * (columns - 2)
    loads = [
        pltpu.make_async_copy(source.at[:, column + m], into.at[m], sems.at[2 * n + m])
        for n, (source, into) in enumerate(((fraction, start), (flow_x, flows), (flow_y, courant)))
        for m in range(2)
    ]
    loads.append(pltpu.make_async_copy(flow_y.at[0], own_y, sems.at[6]))
    loads.append(pltpu.make_async_copy(flow_z.at[:, 0], own_z, sems.at[7]))
    for load in loads:
        load.start()
    for load in loads[:4]:
        load.wait()
    odd = lax.rem(lax.axis_index("row"), 2) == 1
    for m in range(2):
        first[m] = x_sweep_row(start[m], flows[m])
        for i in range(2):
            up, down = first[m, rows - 2 + i : rows - 1 + i], first[m, i : i + 1]
            near[i, m : m + 1] = lax.select(odd, down, up)
            far[i, m : m + 1] = lax.select(odd, up, down)
    for load in loads[4:]:
        load.wait()
    for m in range(2):
        near[2, m : m + 1] = courant[m, :1]
        far[2, m : m + 1] = courant[m, :1]


def x_rows(fraction, flow_x, own_y, high, low, upward, downward):
    rows, columns, _ = fraction.shape
    odd_core = lax.rem(lax.axis_index("col"), 2) == 1
    pairs = columns // 2 - 1

    def put(message, i, row):
        for p in range(pairs):
            message[i * pairs + p] = lax.select(
                odd_core, row[2 * p : 2 * p + 2], row[2 * p + 2 : 2 * p + 4]
            )

    put(downward, 2, own_y[...])
    for mine, message, start in ((low, downward, 0), (high, upward, rows - 2)):
        for i in range(2):
            mine[i] = x_sweep_row(fraction[start + i], flow_x[start + i])
            put(message, i, mine[i])


def x_middle(fraction, flow_x, chip, middle):
    del chip
    for i in range(middle.shape[0]):
        middle[i] = x_sweep_row(fraction[i + 2], flow_x[i + 2])


def y_columns(
    first, start, courant, near, near_side, far, far_side, own_z, chip, own_z_out, lower, upper
):
    _, rows, length = first.shape
    own_z_out[...] = own_z[...]
    odd = lax.rem(lax.axis_index("row"), 2) == 1
    lower[...] = lax.select(odd, near_side[...], far_side[...])
    upper[...] = lax.select(odd, far_side[...], near_side[...])
    place = lax.broadcasted_iota(jnp.int32, (rows, CHUNK), 0)
    bottom = place == 0
    top = place == rows - 1
    for j in range(length // CHUNK):
        at = slice(j * CHUNK, (j + 1) * CHUNK)
        high = [lax.select(odd, far[i, :, at], near[i, :, at]) for i in range(2)]
        last_flux = face_flux(
            *high, upper[0, :, at], upper[1, :, at], upper[2, :, at]
        )
        for m in range(2):
            one = slice(m, m + 1)
            here, flow = first[m, :, at], courant[m, :, at]
            below = jnp.where(bottom, lower[1, one, at], pltpu.roll(here, 1, 0))
            two_below = jnp.where(bottom, lower[0, one, at], pltpu.roll(below, 1, 0))
            above = jnp.where(top, upper[0, one, at], pltpu.roll(here, rows - 1, 0))
            flux = face_flux(two_below, below, here, above, flow)
            next_flux = jnp.where(top, last_flux[one], pltpu.roll(flux, rows - 1, 0))
            next_flow = jnp.where(top, upper[2, one, at], pltpu.roll(flow, rows - 1, 0))
            chip[m, :, at] = updated(here, flux, next_flux, flow, next_flow, start[m, :, at])


def y_sweep(
    high, lower_pairs, low, upper_pairs, lower_edge, upper_edge, middle, flow_y, fraction,
    second, core, halo,
):
    rows, columns, length = second.shape
    odd_core = lax.rem(lax.axis_index("col"), 2) == 1
    pairs = columns // 2 - 1
    for edge, rest, slabs in ((lower_edge, lower_pairs, (0, 1)), (upper_edge, upper_pairs, (2, 3, 4))):
        for m, slab in enumerate(slabs):
            others = [rest[m * pairs + p] for p in range(pairs)]
            ends = [edge[m], *others], [*others, edge[m]]
            for p in range(pairs + 1):
                halo[slab, 2 * p : 2 * p + 2] = lax.select(odd_core, ends[1][p], ends[0][p])

    def tile(t, _):
        at = pl.ds(pl.multiple_of(t * LANES, LANES), LANES)

        def pair(ref, start=0):
            return [ref[start + i, :, at] for i in range(2)]

        inner = [middle[i, :, at] for i in range(rows - 4)]
        cells = pair(halo) + pair(low) + inner + pair(high) + pair(halo, 2)
        flows = [flow_y[i, :, at] for i in range(rows)] + [halo[4, :, at]]
        flux = face_flux(*cells[:4], flows[0])
        for i in range(rows):
            next_flux = face_flux(*cells[i + 1 : i + 5], flows[i + 1])
            result = updated(
                cells[i + 2], flux, next_flux, flows[i], flows[i + 1], fraction[i, :, at]
            )
            flux = next_flux
            second[i, :, at] = result
            for m in range(2):
                up, down = result[columns - 2 + m : columns - 1 + m], result[m : m + 1]
                core[m, i : i + 1, at] = lax.select(odd_core, down, up)
        return _

    lax.fori_loop(0, length // LANES, tile, None, unroll=2)


def z_inner(second, flow_z, fraction, base, inside):
    rows, columns, length = second.shape
    place = lax.broadcasted_iota(jnp.int32, (columns, CHUNK), 0)
    top = place == columns - 1
    inner = (place >= 2) & (place <= columns - 2)
    for i in range(rows):
        for j in range(length // CHUNK):
            at = slice(j * CHUNK, (j + 1) * CHUNK)
            here = second[i, :, at]
            courant = flow_z[i, :, at]
            flux = face_flux(
                pltpu.roll(here, 2, 0),
                pltpu.roll(here, 1, 0),
                here,
                pltpu.roll(here, columns - 1, 0),
                courant,
            )
            flux = jnp.where(inner, flux, 0.0)
            next_courant = jnp.where(top, 0.0, pltpu.roll(courant, columns - 1, 0))
            start = fraction[i, :, at]
            base[i, :, at] = updated(
                here, flux, pltpu.roll(flux, columns - 1, 0), courant, next_courant, start
            )
            inside[4, i : i + 1, at] = start[columns - 1 :]
            inside[0, i : i + 1, at] = here[2:3]
            inside[1, i : i + 1, at] = here[columns - 3 : columns - 2]
            inside[2, i : i + 1, at] = courant[1:2]
            inside[3, i : i + 1, at] = courant[columns - 1 :]


def z_outer(
    chip, chip_side, core, core_side, base, inside, own_z, courant_z, out,
    part, change, sems,
):
    rows, columns, length = base.shape
    odd_core = lax.rem(lax.axis_index("col"), 2) == 1
    place = lax.broadcasted_iota(jnp.int32, (columns, CHUNK), 0)
    pieces = [slice(j * CHUNK, (j + 1) * CHUNK) for j in range(length // CHUNK)]

    for at in pieces:

        def ordered(a, b, at=at):
            pairs = [(a[m, :, at], b[m, :, at]) for m in range(a.shape[0])]
            return [lax.select(odd_core, x, y) for x, y in pairs], [
                lax.select(odd_core, y, x) for x, y in pairs
            ]

        below, above = ordered(core_side, chip_side)
        low, high = ordered(core, chip)
        after_low, before_high = inside[0, :, at], inside[1, :, at]
        flux = [
            face_flux(*below, *low, own_z[:, at]),
            face_flux(below[1], *low, after_low, inside[2, :, at]),
            face_flux(before_high, *high, above[0], inside[3, :, at]),
            face_flux(*high, *above, courant_z[:, at]),
        ]
        change[0, :, at] = flux[0] - flux[1]
        change[1, :, at] = flux[1]
        change[2, :, at] = -flux[2]
        spread = jnp.where(inside[4, :, at] > 0.5, courant_z[:, at], 0.0)
        change[3, :, at] = flux[2] - flux[3] + spread

    stores = []
    for i in range(rows):
        for at in pieces:
            value = jnp.zeros((columns, CHUNK), base.dtype)
            for n, column in enumerate((0, 1, columns - 2, columns - 1)):
                value = jnp.where(place == column, change[n, i : i + 1, at], value)
            part[i, :, at] = base[i, :, at] + value
        stores.append(pltpu.make_async_copy(part.at[i], out.at[i], sems.at[i]))
        stores[-1].start()
    for store in stores:
        store.wait()


def per_device(n_row, n_col, fraction, flow_x, flow_y, flow_z):
    block, dtype = fraction.shape, fraction.dtype
    rows, columns, length = block
    vmem = pl.BlockSpec(memory_space=pltpu.VMEM)
    hbm = pl.BlockSpec(memory_space=pltpu.HBM)
    params = pltpu.CompilerParams(vmem_limit_bytes=16 * 1024 * 1024)
    dma = pltpu.SemaphoreType.DMA
    busy = pl.CostEstimate(flops=10**10, bytes_accessed=10**7, transcendentals=0)

    def array(*shape):
        return jax.ShapeDtypeStruct(shape, dtype)

    def with_above(n):
        return [(i, i ^ 1) for i in range(n)]

    def up(n):
        return [(i, (i + 1) % n) for i in range(n)]

    def down(n):
        return [(i, (i - 1) % n) for i in range(n)]

    def with_below(n):
        return [(i, ((i + 1 ^ 1) - 1) % n) for i in range(n)]

    inputs = [
        pltpu.with_memory_space_constraint(x, pltpu.HBM) for x in (fraction, flow_x, flow_y, flow_z)
    ]
    edge, side = array(2, rows, length), array(3, 2, length)
    first, start, courant, near, far, own_y, own_z = pl.pallas_call(
        x_columns,
        out_shape=(
            edge, edge, edge, side, side, array(columns, length), array(rows, length)
        ),
        in_specs=[hbm] * 4,
        out_specs=[vmem] * 7,
        scratch_shapes=[pltpu.VMEM((2, rows, length), dtype), dma((8,))],
        compiler_params=params,
        name="x_columns",
    )(*inputs)
    near_side = lax.ppermute(near, "row", with_above(n_row))
    far_side = lax.ppermute(far, "row", with_below(n_row))
    pairs = columns // 2 - 1
    high, low, upward_pairs, downward_pairs = pl.pallas_call(
        x_rows,
        out_shape=(
            array(2, columns, length),
            array(2, columns, length),
            array(2 * pairs, 2, length),
            array(3 * pairs, 2, length),
        ),
        in_specs=[vmem] * 3,
        out_specs=[vmem] * 4,
        compiler_params=params,
        cost_estimate=busy,
        name="x_rows",
    )(fraction, flow_x, own_y)
    lower_pairs = lax.ppermute(upward_pairs, "row", up(n_row))
    upper_pairs = lax.ppermute(downward_pairs, "row", down(n_row))
    chip, own_z, column_lower, column_upper = pl.pallas_call(
        y_columns,
        out_shape=(edge, array(rows, length), side, side),
        in_specs=[vmem] * 8,
        out_specs=[vmem] * 4,
        compiler_params=params,
        cost_estimate=busy,
        name="y_columns",
    )(first, start, courant, near, near_side, far, far_side, own_z)
    chip_side = lax.ppermute(chip, "col", with_below(n_col))
    courant_z = lax.ppermute(own_z, "col", down(n_col))
    middle = pl.pallas_call(
        x_middle,
        out_shape=array(rows - 4, columns, length),
        in_specs=[vmem] * 3,
        out_specs=vmem,
        compiler_params=params,
        name="x_middle",
    )(fraction, flow_x, upper_pairs)
    second, core = pl.pallas_call(
        y_sweep,
        out_shape=(array(*block), edge),
        in_specs=[vmem] * 9,
        out_specs=[vmem] * 2,
        scratch_shapes=[pltpu.VMEM((5, columns, length), dtype)],
        compiler_params=params,
        cost_estimate=busy,
        name="y_sweep",
    )(
        high, lower_pairs, low, upper_pairs, column_lower, column_upper, middle, flow_y, fraction
    )
    core_side = lax.ppermute(core, "col", with_above(n_col))
    base, inside = pl.pallas_call(
        z_inner,
        out_shape=(array(*block), array(5, rows, length)),
        in_specs=[vmem] * 3,
        out_specs=[vmem] * 2,
        compiler_params=params,
        cost_estimate=busy,
        name="z_inner",
    )(second, flow_z, fraction)
    return pl.pallas_call(
        z_outer,
        out_shape=array(*block),
        in_specs=[vmem] * 8,
        out_specs=hbm,
        scratch_shapes=[
            pltpu.VMEM(block, dtype),
            pltpu.VMEM((4, rows, length), dtype),
            dma((rows,)),
        ],
        compiler_params=params,
        name="z_outer",
    )(chip, chip_side, core, core_side, base, inside, own_z, courant_z)


def solution(mesh):
    spec = P("row", "col", None)

    def step(fraction, flow_x, flow_y, flow_z):
        return per_device(
            mesh.shape["row"], mesh.shape["col"], fraction, flow_x, flow_y, flow_z
        )

    return jax.shard_map(
        step, mesh=mesh, in_specs=(spec,) * 4, out_specs=spec, check_vma=False
    )
```

```python
import jax
import jax.numpy as jnp
from jax import lax
from jax.experimental import pallas as pl
from jax.experimental.pallas import tpu as pltpu
from jax.sharding import PartitionSpec as P

LANES = 128
CHUNK = 512


def face_flux(two_below, below, here, above, courant):
    forward = courant >= 0.0
    donor = jnp.where(forward, below, here)
    slope = jnp.where(forward, here - two_below, below - above)
    return donor_flux(forward, donor, slope, courant)


def donor_flux(forward, donor, slope, courant):
    reach = jnp.abs(courant)
    least = jnp.minimum(donor, reach)
    most = jnp.maximum(0.0, reach - 1.0 + donor)
    tilt = jnp.tanh(10.0 * slope)
    return jnp.where(forward, 0.5, -0.5) * ((least + most) + tilt * (least - most))


def updated(here, flux, next_flux, courant, next_courant, start):
    spread = jnp.where(start > 0.5, next_courant - courant, 0.0)
    return here - (next_flux - flux) + spread


def x_sweep_row(here, courant):
    length = here.shape[1]
    below = pltpu.roll(here, 1, 1)
    two_below = pltpu.roll(here, 2, 1)
    above = pltpu.roll(here, length - 1, 1)
    flux = face_flux(two_below, below, here, above, courant)
    from_below = flux - jnp.where(below > 0.5, courant, 0.0)
    to_above = flux - jnp.where(here > 0.5, courant, 0.0)
    return here + (to_above - pltpu.roll(from_below, length - 1, 1))


def x_columns(
    fraction, flow_x, flow_y, flow_z, first, start, courant, near, far, own_y, own_z, flows, sems,
):
    rows, columns, _ = fraction.shape
    column = lax.rem(lax.axis_index("col"), 2) * (columns - 2)
    loads = [
        pltpu.make_async_copy(source.at[:, column + m], into.at[m], sems.at[2 * n + m])
        for n, (source, into) in enumerate(((fraction, start), (flow_x, flows), (flow_y, courant)))
        for m in range(2)
    ]
    loads.append(pltpu.make_async_copy(flow_y.at[0], own_y, sems.at[6]))
    loads.append(pltpu.make_async_copy(flow_z.at[:, 0], own_z, sems.at[7]))
    for load in loads:
        load.start()
    for load in loads[:4]:
        load.wait()
    odd = lax.rem(lax.axis_index("row"), 2) == 1
    for m in range(2):
        first[m] = x_sweep_row(start[m], flows[m])
        for i in range(2):
            up, down = first[m, rows - 2 + i : rows - 1 + i], first[m, i : i + 1]
            near[i, m : m + 1] = lax.select(odd, down, up)
            far[i, m : m + 1] = lax.select(odd, up, down)
    for load in loads[4:]:
        load.wait()
    for m in range(2):
        near[2, m : m + 1] = courant[m, :1]
        far[2, m : m + 1] = courant[m, :1]


def x_rows(fraction, flow_x, own_y, high, low, upward, downward):
    rows, columns, _ = fraction.shape
    odd_core = lax.rem(lax.axis_index("col"), 2) == 1
    pairs = columns // 2 - 1

    def put(message, i, row):
        for p in range(pairs):
            message[i * pairs + p] = lax.select(
                odd_core, row[2 * p : 2 * p + 2], row[2 * p + 2 : 2 * p + 4]
            )

    put(downward, 2, own_y[...])
    for mine, message, start in ((low, downward, 0), (high, upward, rows - 2)):
        for i in range(2):
            mine[i] = x_sweep_row(fraction[start + i], flow_x[start + i])
            put(message, i, mine[i])


def x_middle(fraction, flow_x, chip, middle):
    del chip
    for i in range(middle.shape[0]):
        middle[i] = x_sweep_row(fraction[i + 2], flow_x[i + 2])


def y_columns(
    first, start, courant, near, near_side, far, far_side, own_z, chip, own_z_out, lower, upper
):
    _, rows, length = first.shape
    own_z_out[...] = own_z[...]
    odd = lax.rem(lax.axis_index("row"), 2) == 1
    lower[...] = lax.select(odd, near_side[...], far_side[...])
    upper[...] = lax.select(odd, far_side[...], near_side[...])
    place = lax.broadcasted_iota(jnp.int32, (rows, CHUNK), 0)
    bottom = place == 0
    top = place == rows - 1
    for j in range(length // CHUNK):
        at = slice(j * CHUNK, (j + 1) * CHUNK)
        high = [lax.select(odd, far[i, :, at], near[i, :, at]) for i in range(2)]
        last_flux = face_flux(
            *high, upper[0, :, at], upper[1, :, at], upper[2, :, at]
        )
        for m in range(2):
            one = slice(m, m + 1)
            here, flow = first[m, :, at], courant[m, :, at]
            below = jnp.where(bottom, lower[1, one, at], pltpu.roll(here, 1, 0))
            two_below = jnp.where(bottom, lower[0, one, at], pltpu.roll(below, 1, 0))
            above = jnp.where(top, upper[0, one, at], pltpu.roll(here, rows - 1, 0))
            flux = face_flux(two_below, below, here, above, flow)
            next_flux = jnp.where(top, last_flux[one], pltpu.roll(flux, rows - 1, 0))
            next_flow = jnp.where(top, upper[2, one, at], pltpu.roll(flow, rows - 1, 0))
            chip[m, :, at] = updated(here, flux, next_flux, flow, next_flow, start[m, :, at])


def y_sweep(
    high, lower_pairs, low, upper_pairs, lower_edge, upper_edge, middle, flow_y, fraction,
    own_z, second, core, halo,
):
    rows, columns, length = second.shape
    odd_core = lax.rem(lax.axis_index("col"), 2) == 1
    core[2] = own_z[...]
    pairs = columns // 2 - 1
    for edge, rest, slabs in ((lower_edge, lower_pairs, (0, 1)), (upper_edge, upper_pairs, (2, 3, 4))):
        for m, slab in enumerate(slabs):
            others = [rest[m * pairs + p] for p in range(pairs)]
            ends = [edge[m], *others], [*others, edge[m]]
            for p in range(pairs + 1):
                halo[slab, 2 * p : 2 * p + 2] = lax.select(odd_core, ends[1][p], ends[0][p])

    def tile(t, _):
        at = pl.ds(pl.multiple_of(t * LANES, LANES), LANES)

        def pair(ref, start=0):
            return [ref[start + i, :, at] for i in range(2)]

        inner = [middle[i, :, at] for i in range(rows - 4)]
        cells = pair(halo) + pair(low) + inner + pair(high) + pair(halo, 2)
        flows = [flow_y[i, :, at] for i in range(rows)] + [halo[4, :, at]]
        flux = face_flux(*cells[:4], flows[0])
        for i in range(rows):
            next_flux = face_flux(*cells[i + 1 : i + 5], flows[i + 1])
            result = updated(
                cells[i + 2], flux, next_flux, flows[i], flows[i + 1], fraction[i, :, at]
            )
            flux = next_flux
            second[i, :, at] = result
            for m in range(2):
                up, down = result[columns - 2 + m : columns - 1 + m], result[m : m + 1]
                core[m, i : i + 1, at] = lax.select(odd_core, down, up)
        return _

    lax.fori_loop(0, length // LANES, tile, None, unroll=2)


def z_inner(second, flow_z, fraction, out, inside, base, sems):
    rows, columns, length = second.shape
    odd_core = lax.rem(lax.axis_index("col"), 2) == 1
    place = lax.broadcasted_iota(jnp.int32, (columns, CHUNK), 0)
    top = place == columns - 1
    inner = (place >= 2) & (place <= columns - 2)
    stores = []
    for i in range(rows):
        for j in range(length // CHUNK):
            at = slice(j * CHUNK, (j + 1) * CHUNK)
            here = second[i, :, at]
            courant = flow_z[i, :, at]
            flux = face_flux(
                pltpu.roll(here, 2, 0),
                pltpu.roll(here, 1, 0),
                here,
                pltpu.roll(here, columns - 1, 0),
                courant,
            )
            flux = jnp.where(inner, flux, 0.0)
            next_courant = jnp.where(top, 0.0, pltpu.roll(courant, columns - 1, 0))
            start = fraction[i, :, at]
            result = updated(
                here, flux, pltpu.roll(flux, columns - 1, 0), courant, next_courant, start
            )
            base[i, :, at] = result
            inside[4, i : i + 1, at] = start[columns - 1 :]
            for m in range(2):
                upper, lower = result[columns - 2 + m : columns - 1 + m], result[m : m + 1]
                inside[5 + m, i : i + 1, at] = lax.select(odd_core, upper, lower)
                inside[7 + m, i : i + 1, at] = lax.select(odd_core, lower, upper)
            inside[0, i : i + 1, at] = here[2:3]
            inside[1, i : i + 1, at] = here[columns - 3 : columns - 2]
            inside[2, i : i + 1, at] = courant[1:2]
            inside[3, i : i + 1, at] = courant[columns - 1 :]
        stores.append(pltpu.make_async_copy(base.at[i], out.at[i], sems.at[i]))
        stores[-1].start()
    for store in stores:
        store.wait()


def side_change(is_lower, own, side, inside, own_z, last_flow, at):
    mine = [own[m, :, at] for m in range(2)]
    theirs = [side[m, :, at] for m in range(2)]

    def pick(lower, upper):
        return [lax.select(is_lower, x, y) for x, y in zip(lower, upper)]

    outer = face_flux(
        *pick([*theirs, *mine, own_z[:, at]], [inside[1, :, at], *mine, theirs[0], inside[3, :, at]])
    )
    inner = face_flux(
        *pick([theirs[1], *mine, inside[0, :, at], inside[2, :, at]], [*mine, *theirs, last_flow])
    )
    spread = jnp.where(inside[4, :, at] > 0.5, last_flow, 0.0)
    return pick([outer - inner, inner], [-outer, outer - inner + spread])


def z_core(core, core_side, inside, own_z, values):
    odd_core = lax.rem(lax.axis_index("col"), 2) == 1
    for j in range(values.shape[2] // CHUNK):
        at = slice(j * CHUNK, (j + 1) * CHUNK)
        change = side_change(odd_core, core, core_side, inside, own_z, core_side[2, :, at], at)
        for m in range(2):
            values[m, :, at] = inside[7 + m, :, at] + change[m]


def z_chip(chip, chip_side, inside, own_z, courant_z, values, result, out, part, sems):
    del result
    columns, length = out.shape[1:]
    upper_side = lax.rem(lax.axis_index("col"), 2)
    column = upper_side * (columns - 2)
    other = (1 - upper_side) * (columns - 2)
    stores = [
        pltpu.make_async_copy(values.at[m], out.at[:, other + m], sems.at[m]) for m in range(2)
    ]
    for store in stores:
        store.start()
    for j in range(length // CHUNK):
        at = slice(j * CHUNK, (j + 1) * CHUNK)
        change = side_change(
            upper_side == 0, chip, chip_side, inside, own_z, courant_z[:, at], at
        )
        for m in range(2):
            part[m, :, at] = inside[5 + m, :, at] + change[m]
    for m in range(2):
        stores.append(pltpu.make_async_copy(part.at[m], out.at[:, column + m], sems.at[2 + m]))
        stores[-1].start()
    for store in stores:
        store.wait()


def per_device(n_row, n_col, fraction, flow_x, flow_y, flow_z):
    block, dtype = fraction.shape, fraction.dtype
    rows, columns, length = block
    vmem = pl.BlockSpec(memory_space=pltpu.VMEM)
    hbm = pl.BlockSpec(memory_space=pltpu.HBM)
    params = pltpu.CompilerParams(vmem_limit_bytes=16 * 1024 * 1024)
    dma = pltpu.SemaphoreType.DMA
    busy = pl.CostEstimate(flops=10**10, bytes_accessed=10**7, transcendentals=0)

    def array(*shape):
        return jax.ShapeDtypeStruct(shape, dtype)

    def with_above(n):
        return [(i, i ^ 1) for i in range(n)]

    def up(n):
        return [(i, (i + 1) % n) for i in range(n)]

    def down(n):
        return [(i, (i - 1) % n) for i in range(n)]

    def with_below(n):
        return [(i, ((i + 1 ^ 1) - 1) % n) for i in range(n)]

    inputs = [
        pltpu.with_memory_space_constraint(x, pltpu.HBM) for x in (fraction, flow_x, flow_y, flow_z)
    ]
    edge, side = array(2, rows, length), array(3, 2, length)
    first, start, courant, near, far, own_y, own_z = pl.pallas_call(
        x_columns,
        out_shape=(
            edge, edge, edge, side, side, array(columns, length), array(rows, length)
        ),
        in_specs=[hbm] * 4,
        out_specs=[vmem] * 7,
        scratch_shapes=[pltpu.VMEM((2, rows, length), dtype), dma((8,))],
        compiler_params=params,
        name="x_columns",
    )(*inputs)
    near_side = lax.ppermute(near, "row", with_above(n_row))
    far_side = lax.ppermute(far, "row", with_below(n_row))
    pairs = columns // 2 - 1
    high, low, upward_pairs, downward_pairs = pl.pallas_call(
        x_rows,
        out_shape=(
            array(2, columns, length),
            array(2, columns, length),
            array(2 * pairs, 2, length),
            array(3 * pairs, 2, length),
        ),
        in_specs=[vmem] * 3,
        out_specs=[vmem] * 4,
        compiler_params=params,
        cost_estimate=busy,
        name="x_rows",
    )(fraction, flow_x, own_y)
    lower_pairs = lax.ppermute(upward_pairs, "row", up(n_row))
    upper_pairs = lax.ppermute(downward_pairs, "row", down(n_row))
    chip, own_z, column_lower, column_upper = pl.pallas_call(
        y_columns,
        out_shape=(edge, array(rows, length), side, side),
        in_specs=[vmem] * 8,
        out_specs=[vmem] * 4,
        compiler_params=params,
        cost_estimate=busy,
        name="y_columns",
    )(first, start, courant, near, near_side, far, far_side, own_z)
    chip_side = lax.ppermute(chip, "col", with_below(n_col))
    courant_z = lax.ppermute(own_z, "col", down(n_col))
    middle = pl.pallas_call(
        x_middle,
        out_shape=array(rows - 4, columns, length),
        in_specs=[vmem] * 3,
        out_specs=vmem,
        compiler_params=params,
        name="x_middle",
    )(fraction, flow_x, upper_pairs)
    second, core = pl.pallas_call(
        y_sweep,
        out_shape=(array(*block), array(3, rows, length)),
        in_specs=[vmem] * 10,
        out_specs=[vmem] * 2,
        scratch_shapes=[pltpu.VMEM((5, columns, length), dtype)],
        compiler_params=params,
        cost_estimate=busy,
        name="y_sweep",
    )(
        high, lower_pairs, low, upper_pairs, column_lower, column_upper, middle, flow_y, fraction,
        own_z,
    )
    core_side = lax.ppermute(core, "col", with_above(n_col))
    result, inside = pl.pallas_call(
        z_inner,
        out_shape=(array(*block), array(9, rows, length)),
        in_specs=[vmem] * 3,
        out_specs=[hbm, vmem],
        scratch_shapes=[pltpu.VMEM(block, dtype), dma((rows,))],
        compiler_params=params,
        cost_estimate=busy,
        name="z_inner",
    )(second, flow_z, fraction)
    values = pl.pallas_call(
        z_core,
        out_shape=edge,
        in_specs=[vmem] * 4,
        out_specs=vmem,
        compiler_params=params,
        name="z_core",
    )(core, core_side, inside, own_z)
    return pl.pallas_call(
        z_chip,
        out_shape=array(*block),
        in_specs=[vmem] * 6 + [hbm],
        out_specs=hbm,
        scratch_shapes=[pltpu.VMEM((2, rows, length), dtype), dma((4,))],
        input_output_aliases={6: 0},
        compiler_params=params,
        name="z_chip",
    )(chip, chip_side, inside, own_z, courant_z, values, result)


def solution(mesh):
    spec = P("row", "col", None)

    def step(fraction, flow_x, flow_y, flow_z):
        return per_device(
            mesh.shape["row"], mesh.shape["col"], fraction, flow_x, flow_y, flow_z
        )

    return jax.shard_map(
        step, mesh=mesh, in_specs=(spec,) * 4, out_specs=spec, check_vma=False
    )
```

```python
import jax
import jax.numpy as jnp
from jax import lax
from jax.experimental import pallas as pl
from jax.experimental.pallas import tpu as pltpu
from jax.sharding import PartitionSpec as P

LANES = 128
CHUNK = 512


def face_flux(two_below, below, here, above, courant):
    forward = courant >= 0.0
    donor = jnp.where(forward, below, here)
    slope = jnp.where(forward, here - two_below, below - above)
    return donor_flux(forward, donor, slope, courant)


def donor_flux(forward, donor, slope, courant):
    reach = jnp.abs(courant)
    least = jnp.minimum(donor, reach)
    most = jnp.maximum(0.0, reach - 1.0 + donor)
    tilt = jnp.tanh(10.0 * slope)
    return jnp.where(forward, 0.5, -0.5) * ((least + most) + tilt * (least - most))


def updated(here, flux, next_flux, courant, next_courant, start):
    spread = jnp.where(start > 0.5, next_courant - courant, 0.0)
    return here - (next_flux - flux) + spread


def x_sweep_row(here, courant):
    length = here.shape[1]
    below = pltpu.roll(here, 1, 1)
    two_below = pltpu.roll(here, 2, 1)
    above = pltpu.roll(here, length - 1, 1)
    flux = face_flux(two_below, below, here, above, courant)
    from_below = flux - jnp.where(below > 0.5, courant, 0.0)
    to_above = flux - jnp.where(here > 0.5, courant, 0.0)
    return here + (to_above - pltpu.roll(from_below, length - 1, 1))


def x_columns(
    fraction, flow_x, flow_y, flow_z, first, start, courant, near, far, own_y, own_z, flows, sems,
):
    rows, columns, _ = fraction.shape
    column = lax.rem(lax.axis_index("col"), 2) * (columns - 2)
    loads = [
        pltpu.make_async_copy(source.at[:, column + m], into.at[m], sems.at[2 * n + m])
        for n, (source, into) in enumerate(((fraction, start), (flow_x, flows), (flow_y, courant)))
        for m in range(2)
    ]
    loads.append(pltpu.make_async_copy(flow_y.at[0], own_y, sems.at[6]))
    loads.append(pltpu.make_async_copy(flow_z.at[:, 0], own_z, sems.at[7]))
    for load in loads:
        load.start()
    for load in loads[:4]:
        load.wait()
    odd = lax.rem(lax.axis_index("row"), 2) == 1
    for m in range(2):
        first[m] = x_sweep_row(start[m], flows[m])
        for i in range(2):
            up, down = first[m, rows - 2 + i : rows - 1 + i], first[m, i : i + 1]
            near[i, m : m + 1] = lax.select(odd, down, up)
            far[i, m : m + 1] = lax.select(odd, up, down)
    for load in loads[4:]:
        load.wait()
    for m in range(2):
        near[2, m : m + 1] = courant[m, :1]
        far[2, m : m + 1] = courant[m, :1]


def x_rows(fraction, flow_x, own_y, high, low, upward, downward):
    rows, columns, _ = fraction.shape
    odd_core = lax.rem(lax.axis_index("col"), 2) == 1
    pairs = columns // 2 - 1

    def put(message, i, row):
        for p in range(pairs):
            message[i * pairs + p] = lax.select(
                odd_core, row[2 * p : 2 * p + 2], row[2 * p + 2 : 2 * p + 4]
            )

    put(downward, 2, own_y[...])
    for mine, message, start in ((low, downward, 0), (high, upward, rows - 2)):
        for i in range(2):
            mine[i] = x_sweep_row(fraction[start + i], flow_x[start + i])
            put(message, i, mine[i])


def x_middle(fraction, flow_x, chip, middle):
    del chip
    for i in range(middle.shape[0]):
        middle[i] = x_sweep_row(fraction[i + 2], flow_x[i + 2])


def y_columns(
    first, start, courant, near, near_side, far, far_side, own_z, chip, own_z_out, lower, upper
):
    _, rows, length = first.shape
    own_z_out[...] = own_z[...]
    odd = lax.rem(lax.axis_index("row"), 2) == 1
    lower[...] = lax.select(odd, near_side[...], far_side[...])
    upper[...] = lax.select(odd, far_side[...], near_side[...])
    place = lax.broadcasted_iota(jnp.int32, (rows, CHUNK), 0)
    bottom = place == 0
    top = place == rows - 1
    for j in range(length // CHUNK):
        at = slice(j * CHUNK, (j + 1) * CHUNK)
        high = [lax.select(odd, far[i, :, at], near[i, :, at]) for i in range(2)]
        last_flux = face_flux(
            *high, upper[0, :, at], upper[1, :, at], upper[2, :, at]
        )
        for m in range(2):
            one = slice(m, m + 1)
            here, flow = first[m, :, at], courant[m, :, at]
            below = jnp.where(bottom, lower[1, one, at], pltpu.roll(here, 1, 0))
            two_below = jnp.where(bottom, lower[0, one, at], pltpu.roll(below, 1, 0))
            above = jnp.where(top, upper[0, one, at], pltpu.roll(here, rows - 1, 0))
            flux = face_flux(two_below, below, here, above, flow)
            next_flux = jnp.where(top, last_flux[one], pltpu.roll(flux, rows - 1, 0))
            next_flow = jnp.where(top, upper[2, one, at], pltpu.roll(flow, rows - 1, 0))
            chip[m, :, at] = updated(here, flux, next_flux, flow, next_flow, start[m, :, at])


def y_sweep(
    high, lower_pairs, low, upper_pairs, lower_edge, upper_edge, middle, flow_y, fraction,
    own_z, second, core, halo,
):
    rows, columns, length = second.shape
    odd_core = lax.rem(lax.axis_index("col"), 2) == 1
    core[2] = own_z[...]
    pairs = columns // 2 - 1
    for edge, rest, slabs in ((lower_edge, lower_pairs, (0, 1)), (upper_edge, upper_pairs, (2, 3, 4))):
        for m, slab in enumerate(slabs):
            others = [rest[m * pairs + p] for p in range(pairs)]
            ends = [edge[m], *others], [*others, edge[m]]
            for p in range(pairs + 1):
                halo[slab, 2 * p : 2 * p + 2] = lax.select(odd_core, ends[1][p], ends[0][p])

    def tile(t, _):
        at = pl.ds(pl.multiple_of(t * LANES, LANES), LANES)

        def pair(ref, start=0):
            return [ref[start + i, :, at] for i in range(2)]

        inner = [middle[i, :, at] for i in range(rows - 4)]
        cells = pair(halo) + pair(low) + inner + pair(high) + pair(halo, 2)
        flows = [flow_y[i, :, at] for i in range(rows)] + [halo[4, :, at]]
        flux = face_flux(*cells[:4], flows[0])
        for i in range(rows):
            next_flux = face_flux(*cells[i + 1 : i + 5], flows[i + 1])
            result = updated(
                cells[i + 2], flux, next_flux, flows[i], flows[i + 1], fraction[i, :, at]
            )
            flux = next_flux
            second[i, :, at] = result
            for m in range(2):
                up, down = result[columns - 2 + m : columns - 1 + m], result[m : m + 1]
                core[m, i : i + 1, at] = lax.select(odd_core, down, up)
        return _

    lax.fori_loop(0, length // LANES, tile, None, unroll=4)


def z_inner(second, flow_z, fraction, out, inside, base, sems):
    rows, columns, length = second.shape
    odd_core = lax.rem(lax.axis_index("col"), 2) == 1
    place = lax.broadcasted_iota(jnp.int32, (columns, CHUNK), 0)
    top = place == columns - 1
    inner = (place >= 2) & (place <= columns - 2)
    stores = []
    for i in range(rows):
        for j in range(length // CHUNK):
            at = slice(j * CHUNK, (j + 1) * CHUNK)
            here = second[i, :, at]
            courant = flow_z[i, :, at]
            flux = face_flux(
                pltpu.roll(here, 2, 0),
                pltpu.roll(here, 1, 0),
                here,
                pltpu.roll(here, columns - 1, 0),
                courant,
            )
            flux = jnp.where(inner, flux, 0.0)
            next_courant = jnp.where(top, 0.0, pltpu.roll(courant, columns - 1, 0))
            start = fraction[i, :, at]
            result = updated(
                here, flux, pltpu.roll(flux, columns - 1, 0), courant, next_courant, start
            )
            base[i, :, at] = result
            inside[4, i : i + 1, at] = start[columns - 1 :]
            for m in range(2):
                upper, lower = result[columns - 2 + m : columns - 1 + m], result[m : m + 1]
                inside[5 + m, i : i + 1, at] = lax.select(odd_core, upper, lower)
                inside[7 + m, i : i + 1, at] = lax.select(odd_core, lower, upper)
            inside[0, i : i + 1, at] = here[2:3]
            inside[1, i : i + 1, at] = here[columns - 3 : columns - 2]
            inside[2, i : i + 1, at] = courant[1:2]
            inside[3, i : i + 1, at] = courant[columns - 1 :]
        stores.append(pltpu.make_async_copy(base.at[i], out.at[i], sems.at[i]))
        stores[-1].start()
    for store in stores:
        store.wait()


def side_change(is_lower, own, side, inside, own_z, last_flow, at):
    mine = [own[m, :, at] for m in range(2)]
    theirs = [side[m, :, at] for m in range(2)]

    def pick(lower, upper):
        return [lax.select(is_lower, x, y) for x, y in zip(lower, upper)]

    outer = face_flux(
        *pick([*theirs, *mine, own_z[:, at]], [inside[1, :, at], *mine, theirs[0], inside[3, :, at]])
    )
    inner = face_flux(
        *pick([theirs[1], *mine, inside[0, :, at], inside[2, :, at]], [*mine, *theirs, last_flow])
    )
    spread = jnp.where(inside[4, :, at] > 0.5, last_flow, 0.0)
    return pick([outer - inner, inner], [-outer, outer - inner + spread])


def z_core(core, core_side, inside, own_z, values):
    odd_core = lax.rem(lax.axis_index("col"), 2) == 1
    for j in range(values.shape[2] // CHUNK):
        at = slice(j * CHUNK, (j + 1) * CHUNK)
        change = side_change(odd_core, core, core_side, inside, own_z, core_side[2, :, at], at)
        for m in range(2):
            values[m, :, at] = inside[7 + m, :, at] + change[m]


def z_chip(chip, chip_side, inside, own_z, courant_z, values, result, out, part, sems):
    del result
    columns, length = out.shape[1:]
    upper_side = lax.rem(lax.axis_index("col"), 2)
    column = upper_side * (columns - 2)
    other = (1 - upper_side) * (columns - 2)
    stores = [
        pltpu.make_async_copy(values.at[m], out.at[:, other + m], sems.at[m]) for m in range(2)
    ]
    for store in stores:
        store.start()
    for j in range(length // CHUNK):
        at = slice(j * CHUNK, (j + 1) * CHUNK)
        change = side_change(
            upper_side == 0, chip, chip_side, inside, own_z, courant_z[:, at], at
        )
        for m in range(2):
            part[m, :, at] = inside[5 + m, :, at] + change[m]
    for m in range(2):
        stores.append(pltpu.make_async_copy(part.at[m], out.at[:, column + m], sems.at[2 + m]))
        stores[-1].start()
    for store in stores:
        store.wait()


def per_device(n_row, n_col, fraction, flow_x, flow_y, flow_z):
    block, dtype = fraction.shape, fraction.dtype
    rows, columns, length = block
    vmem = pl.BlockSpec(memory_space=pltpu.VMEM)
    hbm = pl.BlockSpec(memory_space=pltpu.HBM)
    params = pltpu.CompilerParams(vmem_limit_bytes=16 * 1024 * 1024)
    dma = pltpu.SemaphoreType.DMA
    busy = pl.CostEstimate(flops=10**10, bytes_accessed=10**7, transcendentals=0)

    def array(*shape):
        return jax.ShapeDtypeStruct(shape, dtype)

    def with_above(n):
        return [(i, i ^ 1) for i in range(n)]

    def up(n):
        return [(i, (i + 1) % n) for i in range(n)]

    def down(n):
        return [(i, (i - 1) % n) for i in range(n)]

    def with_below(n):
        return [(i, ((i + 1 ^ 1) - 1) % n) for i in range(n)]

    inputs = [
        pltpu.with_memory_space_constraint(x, pltpu.HBM) for x in (fraction, flow_x, flow_y, flow_z)
    ]
    edge, side = array(2, rows, length), array(3, 2, length)
    first, start, courant, near, far, own_y, own_z = pl.pallas_call(
        x_columns,
        out_shape=(
            edge, edge, edge, side, side, array(columns, length), array(rows, length)
        ),
        in_specs=[hbm] * 4,
        out_specs=[vmem] * 7,
        scratch_shapes=[pltpu.VMEM((2, rows, length), dtype), dma((8,))],
        compiler_params=params,
        name="x_columns",
    )(*inputs)
    near_side = lax.ppermute(near, "row", with_above(n_row))
    far_side = lax.ppermute(far, "row", with_below(n_row))
    pairs = columns // 2 - 1
    high, low, upward_pairs, downward_pairs = pl.pallas_call(
        x_rows,
        out_shape=(
            array(2, columns, length),
            array(2, columns, length),
            array(2 * pairs, 2, length),
            array(3 * pairs, 2, length),
        ),
        in_specs=[vmem] * 3,
        out_specs=[vmem] * 4,
        compiler_params=params,
        cost_estimate=busy,
        name="x_rows",
    )(fraction, flow_x, own_y)
    lower_pairs = lax.ppermute(upward_pairs, "row", up(n_row))
    upper_pairs = lax.ppermute(downward_pairs, "row", down(n_row))
    chip, own_z, column_lower, column_upper = pl.pallas_call(
        y_columns,
        out_shape=(edge, array(rows, length), side, side),
        in_specs=[vmem] * 8,
        out_specs=[vmem] * 4,
        compiler_params=params,
        cost_estimate=busy,
        name="y_columns",
    )(first, start, courant, near, near_side, far, far_side, own_z)
    chip_side = lax.ppermute(chip, "col", with_below(n_col))
    courant_z = lax.ppermute(own_z, "col", down(n_col))
    middle = pl.pallas_call(
        x_middle,
        out_shape=array(rows - 4, columns, length),
        in_specs=[vmem] * 3,
        out_specs=vmem,
        compiler_params=params,
        name="x_middle",
    )(fraction, flow_x, upper_pairs)
    second, core = pl.pallas_call(
        y_sweep,
        out_shape=(array(*block), array(3, rows, length)),
        in_specs=[vmem] * 10,
        out_specs=[vmem] * 2,
        scratch_shapes=[pltpu.VMEM((5, columns, length), dtype)],
        compiler_params=params,
        cost_estimate=busy,
        name="y_sweep",
    )(
        high, lower_pairs, low, upper_pairs, column_lower, column_upper, middle, flow_y, fraction,
        own_z,
    )
    core_side = lax.ppermute(core, "col", with_above(n_col))
    result, inside = pl.pallas_call(
        z_inner,
        out_shape=(array(*block), array(9, rows, length)),
        in_specs=[vmem] * 3,
        out_specs=[hbm, vmem],
        scratch_shapes=[pltpu.VMEM(block, dtype), dma((rows,))],
        compiler_params=params,
        cost_estimate=busy,
        name="z_inner",
    )(second, flow_z, fraction)
    values = pl.pallas_call(
        z_core,
        out_shape=edge,
        in_specs=[vmem] * 4,
        out_specs=vmem,
        compiler_params=params,
        name="z_core",
    )(core, core_side, inside, own_z)
    return pl.pallas_call(
        z_chip,
        out_shape=array(*block),
        in_specs=[vmem] * 6 + [hbm],
        out_specs=hbm,
        scratch_shapes=[pltpu.VMEM((2, rows, length), dtype), dma((4,))],
        input_output_aliases={6: 0},
        compiler_params=params,
        name="z_chip",
    )(chip, chip_side, inside, own_z, courant_z, values, result)


def solution(mesh):
    spec = P("row", "col", None)

    def step(fraction, flow_x, flow_y, flow_z):
        return per_device(
            mesh.shape["row"], mesh.shape["col"], fraction, flow_x, flow_y, flow_z
        )

    return jax.shard_map(
        step, mesh=mesh, in_specs=(spec,) * 4, out_specs=spec, check_vma=False
    )
```

```python
import jax
import jax.numpy as jnp
from jax import lax
from jax.experimental import pallas as pl
from jax.experimental.pallas import tpu as pltpu
from jax.sharding import PartitionSpec as P

LANES = 128
CHUNK = 512


def face_flux(two_below, below, here, above, courant):
    forward = courant >= 0.0
    donor = jnp.where(forward, below, here)
    slope = jnp.where(forward, here - two_below, below - above)
    return donor_flux(forward, donor, slope, courant)


def donor_flux(forward, donor, slope, courant):
    reach = jnp.abs(courant)
    least = jnp.minimum(donor, reach)
    most = jnp.maximum(0.0, reach - 1.0 + donor)
    tilt = jnp.tanh(10.0 * slope)
    return jnp.where(forward, 0.5, -0.5) * ((least + most) + tilt * (least - most))


def updated(here, flux, next_flux, courant, next_courant, start):
    spread = jnp.where(start > 0.5, next_courant - courant, 0.0)
    return here - (next_flux - flux) + spread


def x_sweep_row(here, courant):
    length = here.shape[1]
    below = pltpu.roll(here, 1, 1)
    two_below = pltpu.roll(here, 2, 1)
    above = pltpu.roll(here, length - 1, 1)
    flux = face_flux(two_below, below, here, above, courant)
    from_below = flux - jnp.where(below > 0.5, courant, 0.0)
    to_above = flux - jnp.where(here > 0.5, courant, 0.0)
    return here + (to_above - pltpu.roll(from_below, length - 1, 1))


def x_columns(
    fraction, flow_x, flow_y, flow_z, first, start, courant, near, far, own_y, own_z, flows, sems,
):
    rows, columns, _ = fraction.shape
    column = lax.rem(lax.axis_index("col"), 2) * (columns - 2)
    loads = [
        pltpu.make_async_copy(source.at[:, column + m], into.at[m], sems.at[2 * n + m])
        for n, (source, into) in enumerate(((fraction, start), (flow_x, flows), (flow_y, courant)))
        for m in range(2)
    ]
    loads.append(pltpu.make_async_copy(flow_y.at[0], own_y, sems.at[6]))
    loads.append(pltpu.make_async_copy(flow_z.at[:, 0], own_z, sems.at[7]))
    for load in loads:
        load.start()
    for load in loads[:4]:
        load.wait()
    odd = lax.rem(lax.axis_index("row"), 2) == 1
    for m in range(2):
        first[m] = x_sweep_row(start[m], flows[m])
        for i in range(2):
            up, down = first[m, rows - 2 + i : rows - 1 + i], first[m, i : i + 1]
            near[i, m : m + 1] = lax.select(odd, down, up)
            far[i, m : m + 1] = lax.select(odd, up, down)
    for load in loads[4:]:
        load.wait()
    for m in range(2):
        near[2, m : m + 1] = courant[m, :1]
        far[2, m : m + 1] = courant[m, :1]


def other_pairs(row):
    odd_core = lax.rem(lax.axis_index("col"), 2) == 1
    return [
        lax.select(odd_core, row[2 * p : 2 * p + 2], row[2 * p + 2 : 2 * p + 4])
        for p in range(row.shape[0] // 2 - 1)
    ]


def x_two_rows(fraction, flow_x, row, mine, message):
    pairs = fraction.shape[1] // 2 - 1
    for i in range(2):
        mine[i] = x_sweep_row(fraction[row + i], flow_x[row + i])
        for p, values in enumerate(other_pairs(mine[i])):
            message[i * pairs + p] = values


def x_high(fraction, flow_x, near_side, high, upward):
    del near_side
    x_two_rows(fraction, flow_x, fraction.shape[0] - 2, high, upward)


def x_low(fraction, flow_x, own_y, low, downward):
    pairs = fraction.shape[1] // 2 - 1
    for p, values in enumerate(other_pairs(own_y[...])):
        downward[2 * pairs + p] = values
    x_two_rows(fraction, flow_x, 0, low, downward)


def x_middle(fraction, flow_x, chip, middle):
    del chip
    for i in range(middle.shape[0]):
        middle[i] = x_sweep_row(fraction[i + 2], flow_x[i + 2])


def y_columns(
    first, start, courant, near, near_side, far, far_side, own_z, chip, own_z_out, lower, upper
):
    _, rows, length = first.shape
    own_z_out[...] = own_z[...]
    odd = lax.rem(lax.axis_index("row"), 2) == 1
    lower[...] = lax.select(odd, near_side[...], far_side[...])
    upper[...] = lax.select(odd, far_side[...], near_side[...])
    place = lax.broadcasted_iota(jnp.int32, (rows, CHUNK), 0)
    bottom = place == 0
    top = place == rows - 1
    for j in range(length // CHUNK):
        at = slice(j * CHUNK, (j + 1) * CHUNK)
        high = [lax.select(odd, far[i, :, at], near[i, :, at]) for i in range(2)]
        last_flux = face_flux(
            *high, upper[0, :, at], upper[1, :, at], upper[2, :, at]
        )
        for m in range(2):
            one = slice(m, m + 1)
            here, flow = first[m, :, at], courant[m, :, at]
            below = jnp.where(bottom, lower[1, one, at], pltpu.roll(here, 1, 0))
            two_below = jnp.where(bottom, lower[0, one, at], pltpu.roll(below, 1, 0))
            above = jnp.where(top, upper[0, one, at], pltpu.roll(here, rows - 1, 0))
            flux = face_flux(two_below, below, here, above, flow)
            next_flux = jnp.where(top, last_flux[one], pltpu.roll(flux, rows - 1, 0))
            next_flow = jnp.where(top, upper[2, one, at], pltpu.roll(flow, rows - 1, 0))
            chip[m, :, at] = updated(here, flux, next_flux, flow, next_flow, start[m, :, at])


def y_sweep(
    high, lower_pairs, low, upper_pairs, lower_edge, upper_edge, middle, flow_y, fraction,
    own_z, second, core, halo,
):
    rows, columns, length = second.shape
    odd_core = lax.rem(lax.axis_index("col"), 2) == 1
    core[2] = own_z[...]
    pairs = columns // 2 - 1
    for edge, rest, slabs in ((lower_edge, lower_pairs, (0, 1)), (upper_edge, upper_pairs, (2, 3, 4))):
        for m, slab in enumerate(slabs):
            others = [rest[m * pairs + p] for p in range(pairs)]
            ends = [edge[m], *others], [*others, edge[m]]
            for p in range(pairs + 1):
                halo[slab, 2 * p : 2 * p + 2] = lax.select(odd_core, ends[1][p], ends[0][p])

    def tile(t, _):
        at = pl.ds(pl.multiple_of(t * LANES, LANES), LANES)

        def pair(ref, start=0):
            return [ref[start + i, :, at] for i in range(2)]

        inner = [middle[i, :, at] for i in range(rows - 4)]
        cells = pair(halo) + pair(low) + inner + pair(high) + pair(halo, 2)
        flows = [flow_y[i, :, at] for i in range(rows)] + [halo[4, :, at]]
        flux = face_flux(*cells[:4], flows[0])
        for i in range(rows):
            next_flux = face_flux(*cells[i + 1 : i + 5], flows[i + 1])
            result = updated(
                cells[i + 2], flux, next_flux, flows[i], flows[i + 1], fraction[i, :, at]
            )
            flux = next_flux
            second[i, :, at] = result
            for m in range(2):
                up, down = result[columns - 2 + m : columns - 1 + m], result[m : m + 1]
                core[m, i : i + 1, at] = lax.select(odd_core, down, up)
        return _

    lax.fori_loop(0, length // LANES, tile, None, unroll=2)


def z_inner(second, flow_z, fraction, out, inside, base, sems):
    rows, columns, length = second.shape
    odd_core = lax.rem(lax.axis_index("col"), 2) == 1
    place = lax.broadcasted_iota(jnp.int32, (columns, CHUNK), 0)
    top = place == columns - 1
    inner = (place >= 2) & (place <= columns - 2)
    stores = []
    for i in range(rows):
        for j in range(length // CHUNK):
            at = slice(j * CHUNK, (j + 1) * CHUNK)
            here = second[i, :, at]
            courant = flow_z[i, :, at]
            flux = face_flux(
                pltpu.roll(here, 2, 0),
                pltpu.roll(here, 1, 0),
                here,
                pltpu.roll(here, columns - 1, 0),
                courant,
            )
            flux = jnp.where(inner, flux, 0.0)
            next_courant = jnp.where(top, 0.0, pltpu.roll(courant, columns - 1, 0))
            start = fraction[i, :, at]
            result = updated(
                here, flux, pltpu.roll(flux, columns - 1, 0), courant, next_courant, start
            )
            base[i, :, at] = result
            inside[4, i : i + 1, at] = start[columns - 1 :]
            for m in range(2):
                upper, lower = result[columns - 2 + m : columns - 1 + m], result[m : m + 1]
                inside[5 + m, i : i + 1, at] = lax.select(odd_core, upper, lower)
                inside[7 + m, i : i + 1, at] = lax.select(odd_core, lower, upper)
            inside[0, i : i + 1, at] = here[2:3]
            inside[1, i : i + 1, at] = here[columns - 3 : columns - 2]
            inside[2, i : i + 1, at] = courant[1:2]
            inside[3, i : i + 1, at] = courant[columns - 1 :]
        stores.append(pltpu.make_async_copy(base.at[i], out.at[i], sems.at[i]))
        stores[-1].start()
    for store in stores:
        store.wait()


def side_change(is_lower, own, side, inside, own_z, last_flow, at):
    mine = [own[m, :, at] for m in range(2)]
    theirs = [side[m, :, at] for m in range(2)]

    def pick(lower, upper):
        return [lax.select(is_lower, x, y) for x, y in zip(lower, upper)]

    outer = face_flux(
        *pick([*theirs, *mine, own_z[:, at]], [inside[1, :, at], *mine, theirs[0], inside[3, :, at]])
    )
    inner = face_flux(
        *pick([theirs[1], *mine, inside[0, :, at], inside[2, :, at]], [*mine, *theirs, last_flow])
    )
    spread = jnp.where(inside[4, :, at] > 0.5, last_flow, 0.0)
    return pick([outer - inner, inner], [-outer, outer - inner + spread])


def z_core(core, core_side, inside, own_z, values):
    odd_core = lax.rem(lax.axis_index("col"), 2) == 1
    for j in range(values.shape[2] // CHUNK):
        at = slice(j * CHUNK, (j + 1) * CHUNK)
        change = side_change(odd_core, core, core_side, inside, own_z, core_side[2, :, at], at)
        for m in range(2):
            values[m, :, at] = inside[7 + m, :, at] + change[m]


def z_chip(chip, chip_side, inside, own_z, courant_z, values, result, out, part, sems):
    del result
    columns, length = out.shape[1:]
    upper_side = lax.rem(lax.axis_index("col"), 2)
    column = upper_side * (columns - 2)
    other = (1 - upper_side) * (columns - 2)
    stores = [
        pltpu.make_async_copy(values.at[m], out.at[:, other + m], sems.at[m]) for m in range(2)
    ]
    for store in stores:
        store.start()
    for j in range(length // CHUNK):
        at = slice(j * CHUNK, (j + 1) * CHUNK)
        change = side_change(
            upper_side == 0, chip, chip_side, inside, own_z, courant_z[:, at], at
        )
        for m in range(2):
            part[m, :, at] = inside[5 + m, :, at] + change[m]
    for m in range(2):
        stores.append(pltpu.make_async_copy(part.at[m], out.at[:, column + m], sems.at[2 + m]))
        stores[-1].start()
    for store in stores:
        store.wait()


def per_device(n_row, n_col, fraction, flow_x, flow_y, flow_z):
    block, dtype = fraction.shape, fraction.dtype
    rows, columns, length = block
    vmem = pl.BlockSpec(memory_space=pltpu.VMEM)
    hbm = pl.BlockSpec(memory_space=pltpu.HBM)
    params = pltpu.CompilerParams(vmem_limit_bytes=16 * 1024 * 1024)
    dma = pltpu.SemaphoreType.DMA
    busy = pl.CostEstimate(flops=10**10, bytes_accessed=10**7, transcendentals=0)

    def array(*shape):
        return jax.ShapeDtypeStruct(shape, dtype)

    def with_above(n):
        return [(i, i ^ 1) for i in range(n)]

    def up(n):
        return [(i, (i + 1) % n) for i in range(n)]

    def down(n):
        return [(i, (i - 1) % n) for i in range(n)]

    def with_below(n):
        return [(i, ((i + 1 ^ 1) - 1) % n) for i in range(n)]

    inputs = [
        pltpu.with_memory_space_constraint(x, pltpu.HBM) for x in (fraction, flow_x, flow_y, flow_z)
    ]
    edge, side = array(2, rows, length), array(3, 2, length)
    first, start, courant, near, far, own_y, own_z = pl.pallas_call(
        x_columns,
        out_shape=(
            edge, edge, edge, side, side, array(columns, length), array(rows, length)
        ),
        in_specs=[hbm] * 4,
        out_specs=[vmem] * 7,
        scratch_shapes=[pltpu.VMEM((2, rows, length), dtype), dma((8,))],
        compiler_params=params,
        name="x_columns",
    )(*inputs)
    near_side = lax.ppermute(near, "row", with_above(n_row))
    far_side = lax.ppermute(far, "row", with_below(n_row))
    pairs = columns // 2 - 1
    low, downward_pairs = pl.pallas_call(
        x_low,
        out_shape=(array(2, columns, length), array(3 * pairs, 2, length)),
        in_specs=[vmem] * 3,
        out_specs=[vmem] * 2,
        compiler_params=params,
        cost_estimate=busy,
        name="x_low",
    )(fraction, flow_x, own_y)
    upper_pairs = lax.ppermute(downward_pairs, "row", down(n_row))
    high, upward_pairs = pl.pallas_call(
        x_high,
        out_shape=(array(2, columns, length), array(2 * pairs, 2, length)),
        in_specs=[vmem] * 3,
        out_specs=[vmem] * 2,
        compiler_params=params,
        cost_estimate=busy,
        name="x_high",
    )(fraction, flow_x, near_side)
    lower_pairs = lax.ppermute(upward_pairs, "row", up(n_row))
    chip, own_z, column_lower, column_upper = pl.pallas_call(
        y_columns,
        out_shape=(edge, array(rows, length), side, side),
        in_specs=[vmem] * 8,
        out_specs=[vmem] * 4,
        compiler_params=params,
        cost_estimate=busy,
        name="y_columns",
    )(first, start, courant, near, near_side, far, far_side, own_z)
    chip_side = lax.ppermute(chip, "col", with_below(n_col))
    courant_z = lax.ppermute(own_z, "col", down(n_col))
    middle = pl.pallas_call(
        x_middle,
        out_shape=array(rows - 4, columns, length),
        in_specs=[vmem] * 3,
        out_specs=vmem,
        compiler_params=params,
        name="x_middle",
    )(fraction, flow_x, upper_pairs)
    second, core = pl.pallas_call(
        y_sweep,
        out_shape=(array(*block), array(3, rows, length)),
        in_specs=[vmem] * 10,
        out_specs=[vmem] * 2,
        scratch_shapes=[pltpu.VMEM((5, columns, length), dtype)],
        compiler_params=params,
        cost_estimate=busy,
        name="y_sweep",
    )(
        high, lower_pairs, low, upper_pairs, column_lower, column_upper, middle, flow_y, fraction,
        own_z,
    )
    core_side = lax.ppermute(core, "col", with_above(n_col))
    result, inside = pl.pallas_call(
        z_inner,
        out_shape=(array(*block), array(9, rows, length)),
        in_specs=[vmem] * 3,
        out_specs=[hbm, vmem],
        scratch_shapes=[pltpu.VMEM(block, dtype), dma((rows,))],
        compiler_params=params,
        cost_estimate=busy,
        name="z_inner",
    )(second, flow_z, fraction)
    values = pl.pallas_call(
        z_core,
        out_shape=edge,
        in_specs=[vmem] * 4,
        out_specs=vmem,
        compiler_params=params,
        name="z_core",
    )(core, core_side, inside, own_z)
    return pl.pallas_call(
        z_chip,
        out_shape=array(*block),
        in_specs=[vmem] * 6 + [hbm],
        out_specs=hbm,
        scratch_shapes=[pltpu.VMEM((2, rows, length), dtype), dma((4,))],
        input_output_aliases={6: 0},
        compiler_params=params,
        name="z_chip",
    )(chip, chip_side, inside, own_z, courant_z, values, result)


def solution(mesh):
    spec = P("row", "col", None)

    def step(fraction, flow_x, flow_y, flow_z):
        return per_device(
            mesh.shape["row"], mesh.shape["col"], fraction, flow_x, flow_y, flow_z
        )

    return jax.shard_map(
        step, mesh=mesh, in_specs=(spec,) * 4, out_specs=spec, check_vma=False
    )
```

```python
import jax
import jax.numpy as jnp
from jax import lax
from jax.experimental import pallas as pl
from jax.experimental.pallas import tpu as pltpu
from jax.sharding import PartitionSpec as P

LANES = 128
CHUNK = 512


def face_flux(two_below, below, here, above, courant):
    forward = courant >= 0.0
    donor = jnp.where(forward, below, here)
    slope = jnp.where(forward, here - two_below, below - above)
    return donor_flux(forward, donor, slope, courant)


def donor_flux(forward, donor, slope, courant):
    reach = jnp.abs(courant)
    least = jnp.minimum(donor, reach)
    most = jnp.maximum(0.0, reach - 1.0 + donor)
    tilt = jnp.tanh(10.0 * slope)
    return jnp.where(forward, 0.5, -0.5) * ((least + most) + tilt * (least - most))


def updated(here, flux, next_flux, courant, next_courant, start):
    spread = jnp.where(start > 0.5, next_courant - courant, 0.0)
    return here - (next_flux - flux) + spread


def x_sweep_row(here, courant):
    length = here.shape[1]
    below = pltpu.roll(here, 1, 1)
    two_below = pltpu.roll(here, 2, 1)
    above = pltpu.roll(here, length - 1, 1)
    flux = face_flux(two_below, below, here, above, courant)
    from_below = flux - jnp.where(below > 0.5, courant, 0.0)
    to_above = flux - jnp.where(here > 0.5, courant, 0.0)
    return here + (to_above - pltpu.roll(from_below, length - 1, 1))


def x_columns(
    fraction, flow_x, flow_y, flow_z, first, start, courant, near, far, own_y, own_z, flows, sems,
):
    rows, columns, _ = fraction.shape
    column = lax.rem(lax.axis_index("col"), 2) * (columns - 2)
    loads = [
        pltpu.make_async_copy(source.at[:, column + m], into.at[m], sems.at[2 * n + m])
        for n, (source, into) in enumerate(((fraction, start), (flow_x, flows), (flow_y, courant)))
        for m in range(2)
    ]
    loads.append(pltpu.make_async_copy(flow_y.at[0], own_y, sems.at[6]))
    loads.append(pltpu.make_async_copy(flow_z.at[:, 0], own_z, sems.at[7]))
    for load in loads:
        load.start()
    for load in loads[:4]:
        load.wait()
    odd = lax.rem(lax.axis_index("row"), 2) == 1
    for m in range(2):
        first[m] = x_sweep_row(start[m], flows[m])
        for i in range(2):
            up, down = first[m, rows - 2 + i : rows - 1 + i], first[m, i : i + 1]
            near[i, m : m + 1] = lax.select(odd, down, up)
            far[i, m : m + 1] = lax.select(odd, up, down)
    for load in loads[4:]:
        load.wait()
    for m in range(2):
        near[2, m : m + 1] = courant[m, :1]
        far[2, m : m + 1] = courant[m, :1]


def other_pairs(row):
    odd_core = lax.rem(lax.axis_index("col"), 2) == 1
    return [
        lax.select(odd_core, row[2 * p : 2 * p + 2], row[2 * p + 2 : 2 * p + 4])
        for p in range(row.shape[0] // 2 - 1)
    ]


def x_two_rows(fraction, flow_x, row, mine, message):
    pairs = fraction.shape[1] // 2 - 1
    for i in range(2):
        mine[i] = x_sweep_row(fraction[row + i], flow_x[row + i])
        for p, values in enumerate(other_pairs(mine[i])):
            message[i * pairs + p] = values


def x_high(fraction, flow_x, near_side, high, upward):
    del near_side
    x_two_rows(fraction, flow_x, fraction.shape[0] - 2, high, upward)


def x_low(fraction, flow_x, own_y, low, downward):
    pairs = fraction.shape[1] // 2 - 1
    for p, values in enumerate(other_pairs(own_y[...])):
        downward[2 * pairs + p] = values
    x_two_rows(fraction, flow_x, 0, low, downward)


def x_middle(fraction, flow_x, chip, middle):
    del chip
    for i in range(middle.shape[0]):
        middle[i] = x_sweep_row(fraction[i + 2], flow_x[i + 2])


def y_columns(
    first, start, courant, near, near_side, far, far_side, own_z, chip, own_z_out, lower, upper
):
    _, rows, length = first.shape
    own_z_out[...] = own_z[...]
    odd = lax.rem(lax.axis_index("row"), 2) == 1
    lower[...] = lax.select(odd, near_side[...], far_side[...])
    upper[...] = lax.select(odd, far_side[...], near_side[...])
    place = lax.broadcasted_iota(jnp.int32, (rows, CHUNK), 0)
    bottom = place == 0
    top = place == rows - 1
    for j in range(length // CHUNK):
        at = slice(j * CHUNK, (j + 1) * CHUNK)
        high = [lax.select(odd, far[i, :, at], near[i, :, at]) for i in range(2)]
        last_flux = face_flux(
            *high, upper[0, :, at], upper[1, :, at], upper[2, :, at]
        )
        for m in range(2):
            one = slice(m, m + 1)
            here, flow = first[m, :, at], courant[m, :, at]
            below = jnp.where(bottom, lower[1, one, at], pltpu.roll(here, 1, 0))
            two_below = jnp.where(bottom, lower[0, one, at], pltpu.roll(below, 1, 0))
            above = jnp.where(top, upper[0, one, at], pltpu.roll(here, rows - 1, 0))
            flux = face_flux(two_below, below, here, above, flow)
            next_flux = jnp.where(top, last_flux[one], pltpu.roll(flux, rows - 1, 0))
            next_flow = jnp.where(top, upper[2, one, at], pltpu.roll(flow, rows - 1, 0))
            chip[m, :, at] = updated(here, flux, next_flux, flow, next_flow, start[m, :, at])


def y_sweep(
    high, lower_pairs, low, upper_pairs, lower_edge, upper_edge, middle, flow_y, fraction,
    own_z, second, core, halo,
):
    rows, columns, length = second.shape
    odd_core = lax.rem(lax.axis_index("col"), 2) == 1
    core[2] = own_z[...]
    pairs = columns // 2 - 1
    for edge, rest, slabs in ((lower_edge, lower_pairs, (0, 1)), (upper_edge, upper_pairs, (2, 3, 4))):
        for m, slab in enumerate(slabs):
            others = [rest[m * pairs + p] for p in range(pairs)]
            ends = [edge[m], *others], [*others, edge[m]]
            for p in range(pairs + 1):
                halo[slab, 2 * p : 2 * p + 2] = lax.select(odd_core, ends[1][p], ends[0][p])

    def tile(t, _):
        at = pl.ds(pl.multiple_of(t * LANES, LANES), LANES)

        def pair(ref, start=0):
            return [ref[start + i, :, at] for i in range(2)]

        inner = [middle[i, :, at] for i in range(rows - 4)]
        cells = pair(halo) + pair(low) + inner + pair(high) + pair(halo, 2)
        flows = [flow_y[i, :, at] for i in range(rows)] + [halo[4, :, at]]
        flux = face_flux(*cells[:4], flows[0])
        for i in range(rows):
            next_flux = face_flux(*cells[i + 1 : i + 5], flows[i + 1])
            result = updated(
                cells[i + 2], flux, next_flux, flows[i], flows[i + 1], fraction[i, :, at]
            )
            flux = next_flux
            second[i, :, at] = result
            for m in range(2):
                up, down = result[columns - 2 + m : columns - 1 + m], result[m : m + 1]
                core[m, i : i + 1, at] = lax.select(odd_core, down, up)
        return _

    lax.fori_loop(0, length // LANES, tile, None, unroll=4)


def z_inner(second, flow_z, fraction, out, inside, base, sems):
    rows, columns, length = second.shape
    odd_core = lax.rem(lax.axis_index("col"), 2) == 1
    place = lax.broadcasted_iota(jnp.int32, (columns, CHUNK), 0)
    top = place == columns - 1
    inner = (place >= 2) & (place <= columns - 2)
    stores = []
    for i in range(rows):
        for j in range(length // CHUNK):
            at = slice(j * CHUNK, (j + 1) * CHUNK)
            here = second[i, :, at]
            courant = flow_z[i, :, at]
            flux = face_flux(
                pltpu.roll(here, 2, 0),
                pltpu.roll(here, 1, 0),
                here,
                pltpu.roll(here, columns - 1, 0),
                courant,
            )
            flux = jnp.where(inner, flux, 0.0)
            next_courant = jnp.where(top, 0.0, pltpu.roll(courant, columns - 1, 0))
            start = fraction[i, :, at]
            result = updated(
                here, flux, pltpu.roll(flux, columns - 1, 0), courant, next_courant, start
            )
            base[i, :, at] = result
            inside[4, i : i + 1, at] = start[columns - 1 :]
            for m in range(2):
                upper, lower = result[columns - 2 + m : columns - 1 + m], result[m : m + 1]
                inside[5 + m, i : i + 1, at] = lax.select(odd_core, upper, lower)
                inside[7 + m, i : i + 1, at] = lax.select(odd_core, lower, upper)
            inside[0, i : i + 1, at] = here[2:3]
            inside[1, i : i + 1, at] = here[columns - 3 : columns - 2]
            inside[2, i : i + 1, at] = courant[1:2]
            inside[3, i : i + 1, at] = courant[columns - 1 :]
        stores.append(pltpu.make_async_copy(base.at[i], out.at[i], sems.at[i]))
        stores[-1].start()
    for store in stores:
        store.wait()


def side_change(is_lower, own, side, inside, own_z, last_flow, at):
    mine = [own[m, :, at] for m in range(2)]
    theirs = [side[m, :, at] for m in range(2)]

    def pick(lower, upper):
        return [lax.select(is_lower, x, y) for x, y in zip(lower, upper)]

    outer = face_flux(
        *pick([*theirs, *mine, own_z[:, at]], [inside[1, :, at], *mine, theirs[0], inside[3, :, at]])
    )
    inner = face_flux(
        *pick([theirs[1], *mine, inside[0, :, at], inside[2, :, at]], [*mine, *theirs, last_flow])
    )
    spread = jnp.where(inside[4, :, at] > 0.5, last_flow, 0.0)
    return pick([outer - inner, inner], [-outer, outer - inner + spread])


def z_core(core, core_side, inside, own_z, values):
    odd_core = lax.rem(lax.axis_index("col"), 2) == 1
    for j in range(values.shape[2] // CHUNK):
        at = slice(j * CHUNK, (j + 1) * CHUNK)
        change = side_change(odd_core, core, core_side, inside, own_z, core_side[2, :, at], at)
        for m in range(2):
            values[m, :, at] = inside[7 + m, :, at] + change[m]


def z_chip(chip, chip_side, inside, own_z, courant_z, values, result, out, part, sems):
    del result
    columns, length = out.shape[1:]
    upper_side = lax.rem(lax.axis_index("col"), 2)
    column = upper_side * (columns - 2)
    other = (1 - upper_side) * (columns - 2)
    stores = [
        pltpu.make_async_copy(values.at[m], out.at[:, other + m], sems.at[m]) for m in range(2)
    ]
    for store in stores:
        store.start()
    for j in range(length // CHUNK):
        at = slice(j * CHUNK, (j + 1) * CHUNK)
        change = side_change(
            upper_side == 0, chip, chip_side, inside, own_z, courant_z[:, at], at
        )
        for m in range(2):
            part[m, :, at] = inside[5 + m, :, at] + change[m]
    for m in range(2):
        stores.append(pltpu.make_async_copy(part.at[m], out.at[:, column + m], sems.at[2 + m]))
        stores[-1].start()
    for store in stores:
        store.wait()


def per_device(n_row, n_col, fraction, flow_x, flow_y, flow_z):
    block, dtype = fraction.shape, fraction.dtype
    rows, columns, length = block
    vmem = pl.BlockSpec(memory_space=pltpu.VMEM)
    hbm = pl.BlockSpec(memory_space=pltpu.HBM)
    params = pltpu.CompilerParams(vmem_limit_bytes=16 * 1024 * 1024)
    dma = pltpu.SemaphoreType.DMA
    busy = pl.CostEstimate(flops=10**10, bytes_accessed=10**7, transcendentals=0)

    def array(*shape):
        return jax.ShapeDtypeStruct(shape, dtype)

    def with_above(n):
        return [(i, i ^ 1) for i in range(n)]

    def up(n):
        return [(i, (i + 1) % n) for i in range(n)]

    def down(n):
        return [(i, (i - 1) % n) for i in range(n)]

    def with_below(n):
        return [(i, ((i + 1 ^ 1) - 1) % n) for i in range(n)]

    inputs = [
        pltpu.with_memory_space_constraint(x, pltpu.HBM) for x in (fraction, flow_x, flow_y, flow_z)
    ]
    edge, side = array(2, rows, length), array(3, 2, length)
    first, start, courant, near, far, own_y, own_z = pl.pallas_call(
        x_columns,
        out_shape=(
            edge, edge, edge, side, side, array(columns, length), array(rows, length)
        ),
        in_specs=[hbm] * 4,
        out_specs=[vmem] * 7,
        scratch_shapes=[pltpu.VMEM((2, rows, length), dtype), dma((8,))],
        compiler_params=params,
        name="x_columns",
    )(*inputs)
    near_side = lax.ppermute(near, "row", with_above(n_row))
    far_side = lax.ppermute(far, "row", with_below(n_row))
    pairs = columns // 2 - 1
    low, downward_pairs = pl.pallas_call(
        x_low,
        out_shape=(array(2, columns, length), array(3 * pairs, 2, length)),
        in_specs=[vmem] * 3,
        out_specs=[vmem] * 2,
        compiler_params=params,
        cost_estimate=busy,
        name="x_low",
    )(fraction, flow_x, own_y)
    upper_pairs = lax.ppermute(downward_pairs, "row", down(n_row))
    high, upward_pairs = pl.pallas_call(
        x_high,
        out_shape=(array(2, columns, length), array(2 * pairs, 2, length)),
        in_specs=[vmem] * 3,
        out_specs=[vmem] * 2,
        compiler_params=params,
        cost_estimate=busy,
        name="x_high",
    )(fraction, flow_x, near_side)
    lower_pairs = lax.ppermute(upward_pairs, "row", up(n_row))
    chip, own_z, column_lower, column_upper = pl.pallas_call(
        y_columns,
        out_shape=(edge, array(rows, length), side, side),
        in_specs=[vmem] * 8,
        out_specs=[vmem] * 4,
        compiler_params=params,
        cost_estimate=busy,
        name="y_columns",
    )(first, start, courant, near, near_side, far, far_side, own_z)
    chip_side = lax.ppermute(chip, "col", with_below(n_col))
    courant_z = lax.ppermute(own_z, "col", down(n_col))
    middle = pl.pallas_call(
        x_middle,
        out_shape=array(rows - 4, columns, length),
        in_specs=[vmem] * 3,
        out_specs=vmem,
        compiler_params=params,
        name="x_middle",
    )(fraction, flow_x, upper_pairs)
    second, core = pl.pallas_call(
        y_sweep,
        out_shape=(array(*block), array(3, rows, length)),
        in_specs=[vmem] * 10,
        out_specs=[vmem] * 2,
        scratch_shapes=[pltpu.VMEM((5, columns, length), dtype)],
        compiler_params=params,
        cost_estimate=busy,
        name="y_sweep",
    )(
        high, lower_pairs, low, upper_pairs, column_lower, column_upper, middle, flow_y, fraction,
        own_z,
    )
    core_side = lax.ppermute(core, "col", with_above(n_col))
    result, inside = pl.pallas_call(
        z_inner,
        out_shape=(array(*block), array(9, rows, length)),
        in_specs=[vmem] * 3,
        out_specs=[hbm, vmem],
        scratch_shapes=[pltpu.VMEM(block, dtype), dma((rows,))],
        compiler_params=params,
        cost_estimate=busy,
        name="z_inner",
    )(second, flow_z, fraction)
    values = pl.pallas_call(
        z_core,
        out_shape=edge,
        in_specs=[vmem] * 4,
        out_specs=vmem,
        compiler_params=params,
        name="z_core",
    )(core, core_side, inside, own_z)
    return pl.pallas_call(
        z_chip,
        out_shape=array(*block),
        in_specs=[vmem] * 6 + [hbm],
        out_specs=hbm,
        scratch_shapes=[pltpu.VMEM((2, rows, length), dtype), dma((4,))],
        input_output_aliases={6: 0},
        compiler_params=params,
        name="z_chip",
    )(chip, chip_side, inside, own_z, courant_z, values, result)


def solution(mesh):
    spec = P("row", "col", None)

    def step(fraction, flow_x, flow_y, flow_z):
        return per_device(
            mesh.shape["row"], mesh.shape["col"], fraction, flow_x, flow_y, flow_z
        )

    return jax.shard_map(
        step, mesh=mesh, in_specs=(spec,) * 4, out_specs=spec, check_vma=False
    )
```
